32 devices in a mesh: grp: 4 (over y, x), dev: 8 (over z, core).
Axes of the slice: x: 2, y: 2, z: 4, core: 2. Of those that a mesh axis runs over, the one named last changes fastest.
Arguments:
- points: float32 [3, 32768], P(None, ('grp', 'dev')), may hold values from 0 to 2
- charges: float32 [16, 32768], P(None, ('grp', 'dev')), may hold values from -6 to 6
- morton: int32 [32768], P(('grp', 'dev')), may hold values from 0 to 1023, as said below
- neighbours: int32 [128, 8], P(('grp', 'dev')), may hold values from 0 to 127, as said below
- counts: int32 [128], P(('grp', 'dev')), may hold values from 1 to 8
- skel_leaf: float32 [3, 32768], P(None, ('grp', 'dev')), may hold values from 0 to 2
- skel_block: float32 [3, 8192], P(None, ('grp', 'dev')), may hold values from 0 to 2
- skel_group: float32 [3, 1024], replicated, may hold values from 0 to 2
Outputs:
- potential: float32 [16, 32768], P(None, ('grp', 'dev'))
The draws below stay inside these ranges and needn't reach their ends.
Inputs may be any that keep to these rules, and one draw needn't show every extreme that they name: `morton`: each aligned run of 1024 entries is a permutation of 0 to 1023. `neighbours`: entry [q, k] is a leaf other than q, at most 4 leaves away from q; only slots k < counts[q] are used.
All inputs are finite; a program needn't handle non-finite values.
Results may differ from the reference program's by a relative error of at most 0.0003.
Values sent between devices are 32-bit elements; how exact they have to be, the bound alone decides.
A program may use at most 64 MiB of HBM per device.

```python
import math
import jax
import jax.numpy as jnp
from jax import lax

P_SIZE = 256
R = 256
NBR = 8
LEAF_DEV = 4
NRHS = 16
GROUPS = 4
BLOCKS_GRP = 8
BLOCKS = 32
LEAVES = 128
NPTS = 32768


def neighbour_tables(key):
    leaf_total = NPTS // P_SIZE
    subkeys = jax.random.split(jax.random.fold_in(key, 11), 4)
    offsets = jnp.concatenate([jnp.arange(1, LEAF_DEV + 1), -jnp.arange(1, LEAF_DEV + 1)]).astype(jnp.int32)
    orders = jax.vmap(lambda leaf_key: jax.random.permutation(leaf_key, 2 * LEAF_DEV))(jax.random.split(subkeys[0], leaf_total))
    chosen = offsets[orders[:, :NBR]]
    own_leaf = jnp.arange(leaf_total, dtype=jnp.int32)[:, None]
    forward = own_leaf + chosen
    inside = (forward >= 0) & (forward < leaf_total)
    neighbour_ids = jnp.where(inside, forward, own_leaf - chosen).astype(jnp.int32)
    neighbour_ids = neighbour_ids.at[leaf_total - 2, 0].set(leaf_total - 1).at[1, 0].set(0)
    amounts = jax.random.randint(subkeys[1], (leaf_total,), 1, NBR + 1)
    fullest = jax.random.randint(subkeys[2], (), 0, leaf_total)
    emptiest = (fullest + 1 + jax.random.randint(subkeys[3], (), 0, leaf_total - 1)) % leaf_total
    amounts = amounts.at[fullest].set(NBR).at[emptiest].set(1)
    return (neighbour_ids.astype(jnp.int32), amounts.astype(jnp.int32))


def draw_neighbours(key, part):
    return neighbour_tables(key)[0]


def draw_counts(key, part):
    return neighbour_tables(key)[1]


def morton_order(key):
    block_pts = LEAF_DEV * P_SIZE
    subkeys = jax.random.split(jax.random.fold_in(key, 5), NPTS // block_pts)
    orders = jax.vmap(lambda block_key: jax.random.permutation(block_key, block_pts))(subkeys)
    return orders.reshape(-1).astype(jnp.int32)


def draw_morton(key, part):
    return morton_order(key)


def extent_of_cloud():
    return 2.0


def draw_points(key, part):
    leaf_total = NPTS // P_SIZE
    leaf_half = 0.6
    extent = extent_of_cloud()
    subkeys = jax.random.split(jax.random.fold_in(key, 23), 4)
    group_pos = jax.random.uniform(subkeys[0], (3, GROUPS), jnp.float32)
    block_pos = jax.random.uniform(subkeys[1], (3, BLOCKS), jnp.float32)
    leaf_pos = jax.random.uniform(subkeys[2], (3, leaf_total), jnp.float32)
    blended = 0.5 * jnp.repeat(group_pos, BLOCKS_GRP * LEAF_DEV, axis=1) + 0.3 * jnp.repeat(block_pos, LEAF_DEV, axis=1) + 0.2 * leaf_pos
    centres = leaf_half + (extent - 2.0 * leaf_half) * blended
    offsets = jax.random.uniform(subkeys[3], (3, leaf_total, P_SIZE), jnp.float32, -1.0, 1.0)
    sorted_pts = (centres[:, :, None] + leaf_half * offsets).reshape(3, NPTS)
    block_pts = LEAF_DEV * P_SIZE
    block_start = jnp.arange(NPTS, dtype=jnp.int32) // block_pts * block_pts
    source_idx = (block_start + morton_order(key)).astype(jnp.int32)
    return jnp.zeros((3, NPTS), jnp.float32).at[:, source_idx].set(sorted_pts)


def draw_skel_leaf(key, part):
    fraction = jax.random.uniform(jax.random.fold_in(key, 31), (3, LEAVES * R), jnp.float32)
    return extent_of_cloud() * fraction


def draw_skel_block(key, part):
    fraction = jax.random.uniform(jax.random.fold_in(key, 37), (3, BLOCKS * R), jnp.float32)
    return extent_of_cloud() * fraction


def draw_skel_group(key, part):
    fraction = jax.random.uniform(jax.random.fold_in(key, 41), (3, GROUPS * R), jnp.float32)
    return extent_of_cloud() * fraction


def shard_levels(key, shape, shards, smallest, largest):
    level, own = 1.0, jax.random.fold_in(key, 6)
    for dim, parts in shards:
        steps = jnp.exp(jax.random.uniform(jax.random.fold_in(own, dim), (parts,), jnp.float32, smallest / len(shards), largest / len(shards)))
        level = level * jnp.repeat(steps, shape[dim] // parts).reshape([-1 if axis == dim else 1 for axis in range(len(shape))])
    return level


def noise(stream_key, shape, scale, most, cuts=(), held_as=jnp.bfloat16):
    array = scale * jax.random.normal(stream_key, shape, jnp.float32)
    if cuts:
        array = array * shard_levels(stream_key, shape, cuts, -0.22, 0.18)
    return jnp.clip(array, -most, most).astype(held_as)


def setup_inputs(seed: int = 0) -> dict:
    arg_keys = jax.random.split(jax.random.key(seed), 9)
    points = draw_points(jax.random.fold_in(arg_keys[8], 71), 0)
    charges = noise(arg_keys[1], (NRHS, NPTS), 1.0, 6.0, ((1, 32),), jnp.float32)
    morton = draw_morton(jax.random.fold_in(arg_keys[8], 71), 0)
    neighbours = draw_neighbours(jax.random.fold_in(arg_keys[8], 71), 0)
    counts = draw_counts(jax.random.fold_in(arg_keys[8], 71), 0)
    skel_leaf = draw_skel_leaf(jax.random.fold_in(arg_keys[8], 71), 0)
    skel_block = draw_skel_block(jax.random.fold_in(arg_keys[8], 71), 0)
    skel_group = draw_skel_group(jax.random.fold_in(arg_keys[8], 71), 0)
    return {"points": points, "charges": charges, "morton": morton, "neighbours": neighbours, "counts": counts, "skel_leaf": skel_leaf, "skel_block": skel_block, "skel_group": skel_group}


width_sq = 0.1
gain_factor = 5.0

def kernel_tile(source, target):
    distance = (source[0][:, None] - target[0][None, :]) ** 2
    distance = distance + (source[1][:, None] - target[1][None, :]) ** 2
    distance = distance + (source[2][:, None] - target[2][None, :]) ** 2
    return jnp.exp(-distance / width_sq)

def translate(values, source, target, term_count):
    product = jnp.dot(values, kernel_tile(source, target), precision=lax.Precision.HIGHEST, preferred_element_type=jnp.float32)
    return gain_factor / math.sqrt(term_count) * product

def by_leaf(matrix, leading, number, length):
    return matrix.reshape(leading, number, length).transpose(1, 0, 2)

def reference(points, charges, morton, neighbours, counts, skel_leaf, skel_block, skel_group):
    block_pts = LEAF_DEV * P_SIZE
    block_start = jnp.arange(NPTS, dtype=jnp.int32) // block_pts * block_pts
    source_idx = (block_start + morton).astype(jnp.int32)
    sorted_pts = jnp.take(points, source_idx, axis=1)
    sorted_chg = jnp.take(charges, source_idx, axis=1)
    leaf_pts = by_leaf(sorted_pts, 3, LEAVES, P_SIZE)
    leaf_chg = by_leaf(sorted_chg, NRHS, LEAVES, P_SIZE)
    leaf_skel = by_leaf(skel_leaf, 3, LEAVES, R)
    block_skel = by_leaf(skel_block, 3, BLOCKS, R)
    group_skel = by_leaf(skel_group, 3, GROUPS, R)
    leaf_weights = lax.map(lambda inputs: translate(inputs[0], inputs[1], inputs[2], P_SIZE), (leaf_chg, leaf_pts, leaf_skel))
    owner_block = jnp.arange(LEAVES, dtype=jnp.int32) // LEAF_DEV
    lifted = lax.map(lambda inputs: translate(inputs[0], inputs[1], inputs[2], LEAF_DEV * R), (leaf_weights, leaf_skel, block_skel[owner_block]))
    block_weights = lifted.reshape(BLOCKS, LEAF_DEV, NRHS, R).sum(axis=1)
    parent = jnp.arange(BLOCKS, dtype=jnp.int32) // BLOCKS_GRP
    raised = lax.map(lambda inputs: translate(inputs[0], inputs[1], inputs[2], BLOCKS_GRP * R), (block_weights, block_skel, group_skel[parent]))
    group_weights = raised.reshape(GROUPS, BLOCKS_GRP, NRHS, R).sum(axis=1)

    def group_far(target_id):
        keep_mask = (jnp.arange(GROUPS, dtype=jnp.int32) != target_id).astype(jnp.float32)
        masked = (group_weights * keep_mask[:, None, None]).transpose(1, 0, 2).reshape(NRHS, GROUPS * R)
        return translate(masked, skel_group, group_skel[target_id], (GROUPS - 1) * R)
    group_field = lax.map(group_far, jnp.arange(GROUPS, dtype=jnp.int32))

    def block_far(block_id):
        group_id = block_id // BLOCKS_GRP
        first_block = (group_id * BLOCKS_GRP).astype(jnp.int32)
        members = lax.dynamic_slice_in_dim(block_weights, first_block, BLOCKS_GRP, 0)
        keep_mask = (jnp.arange(BLOCKS_GRP, dtype=jnp.int32) + first_block != block_id).astype(jnp.float32)
        masked = (members * keep_mask[:, None, None]).transpose(1, 0, 2).reshape(NRHS, BLOCKS_GRP * R)
        sources = lax.dynamic_slice_in_dim(skel_block, (first_block * R).astype(jnp.int32), BLOCKS_GRP * R, 1)
        target = block_skel[block_id]
        peer_sum = translate(masked, sources, target, (BLOCKS_GRP - 1) * R)
        return peer_sum + translate(group_field[group_id], group_skel[group_id], target, R)
    block_field = lax.map(block_far, jnp.arange(BLOCKS, dtype=jnp.int32))
    leaf_field = lax.map(lambda inputs: translate(inputs[0], inputs[1], inputs[2], R), (block_field[owner_block], block_skel[owner_block], leaf_skel))

    def near_leaf(leaf_id):
        own_pts = leaf_pts[leaf_id]
        direct = translate(leaf_chg[leaf_id], own_pts, own_pts, P_SIZE)

        def one_slot(slot_index, running):
            neighbour = neighbours[leaf_id, slot_index]
            tile_term = translate(leaf_chg[neighbour], leaf_pts[neighbour], own_pts, P_SIZE)
            return running + jnp.where(slot_index < counts[leaf_id], tile_term, jnp.zeros_like(tile_term))
        direct = lax.fori_loop(0, NBR, one_slot, direct)
        return direct + translate(leaf_field[leaf_id], leaf_skel[leaf_id], own_pts, R)
    potential = lax.map(near_leaf, jnp.arange(LEAVES, dtype=jnp.int32))
    return potential.transpose(1, 0, 2).reshape(NRHS, NPTS)
```

```python
import functools
import math

import jax
import jax.numpy as jnp
from jax import lax
from jax.experimental import pallas as pl
from jax.experimental.pallas import tpu as pltpu
from jax.sharding import PartitionSpec as P

width_sq = 0.1
gain_factor = 5.0
to_base_two = math.sqrt(math.log2(math.e) / width_sq)
middle = 1.0
FEAT = 64
ROWS = 8
MESH = pl.DeviceIdType.MESH
f32, bf16 = jnp.float32, jnp.bfloat16


def parts(x, count):
    out = []
    for _ in range(count - 1):
        out.append(x.astype(bf16).astype(f32))
        x = x - out[-1]
    out.append(x.astype(bf16).astype(f32))
    return out


def features(coords):
    row = lax.broadcasted_iota(jnp.int32, coords.shape, 0)
    c = jnp.where(row < 3, (coords - middle) * to_base_two, 0.0)
    norm = jnp.broadcast_to(jnp.sum(c * c, axis=0, keepdims=True), c.shape)
    hi, mid, lo = parts(c, 3)
    n0, n1, n2 = parts(norm, 3)
    one = jnp.ones_like(c)
    zero = jnp.zeros_like(c)
    first = jnp.where(row == 0, n0, jnp.where(row == 1, n1, n2))
    second = jnp.where(row == 3, n0, jnp.where(row == 4, n1, n2))
    src_n = jnp.where(row < 3, first, jnp.where(row < 6, one, zero))
    tgt_n = jnp.where(row < 3, -one, jnp.where(row < 6, -second, zero))
    hi2, mid2, lo2 = hi + hi, mid + mid, lo + lo
    src = jnp.concatenate([hi, hi, mid, mid, hi, lo, src_n, zero], axis=0)
    tgt = jnp.concatenate([hi2, mid2, hi2, mid2, lo2, hi2, tgt_n, zero], axis=0)
    return src, tgt


def split_rows(v):
    return jnp.concatenate(parts(v, 2), axis=0).astype(bf16)


def apply_kernel(v2, src, tgt):
    half = v2.shape[0] // 2
    k = jnp.exp2(jnp.dot(src, tgt, preferred_element_type=f32))
    k_hi = k.astype(bf16)
    k_lo = (k - k_hi.astype(f32)).astype(bf16)
    r = jnp.dot(v2, k_hi, preferred_element_type=f32)
    return r[:half] + r[half:] + jnp.dot(v2[:half], k_lo, preferred_element_type=f32)


def kernel(
    n_groups, n_blocks, leaf_count, leaf_size, rank, slots,
    points, charges, morton, neighbours, counts, skel_leaf, skel_block, skel_group,
    out,
    pad, halo_out, halo_left, halo_right, skel_all, bw_all, gw_all,
    ext_src, ext_v, own_tgt, leaf_src, leaf_tgt, grp_src, blk_src, two_tgt,
    halo_send, halo_recv, skel_send, skel_recv, bw_send, bw_recv, gw_send, gw_recv,
):
    vectors = charges.shape[0]
    block_pts = leaf_count * leaf_size
    g = lax.axis_index("grp")
    m = lax.axis_index("dev")
    block = g * n_blocks + m
    total = n_groups * n_blocks
    right = lax.rem(block + 1, total)
    left = lax.rem(block + total - 1, total)
    right_id = (right // n_blocks, lax.rem(right, n_blocks))
    left_id = (left // n_blocks, lax.rem(left, n_blocks))
    peers = [(g, lax.rem(m + d, n_blocks)) for d in range(1, n_blocks)]
    cousins = [(lax.rem(g + d, n_groups), m) for d in range(1, n_groups)]

    barrier = pltpu.get_barrier_semaphore()
    greeted = [left_id, right_id] + peers + cousins
    for who in greeted:
        pl.semaphore_signal(barrier, inc=1, device_id=who, device_id_type=MESH)

    def scale(terms):
        return gain_factor / math.sqrt(terms)

    pad[...] = jnp.zeros_like(pad)
    pad[0:3, 0:block_pts] = points[...]
    pts = pad[:, 0:block_pts]
    pad[0:3, 0:rank] = skel_block[...]
    skel_all[pl.ds(m, 1)] = pad[:, 0:rank][None]

    stacked = jnp.concatenate(
        parts(pts, 3) + [jnp.zeros_like(pts)] + parts(charges[...], 2), axis=0
    ).astype(bf16)
    place = lax.broadcasted_iota(jnp.int32, (block_pts, leaf_size), 0)
    for i in range(leaf_count):
        cols = slice(i * leaf_size, (i + 1) * leaf_size)
        onehot = jnp.where(place == morton[0:1, cols], 1.0, 0.0).astype(bf16)
        s = jnp.dot(stacked, onehot, preferred_element_type=f32)
        own = s[0:8] + s[8:16] + s[16:24]
        halo_out[0:ROWS, cols] = own
        halo_out[ROWS:, cols] = s[32 : 32 + vectors] + s[32 + vectors :]
        ext_v[leaf_count + i] = s[32:].astype(bf16)

    pl.semaphore_wait(barrier, len(greeted))

    def to_peer(buf, send, recv, k, who, slot):
        return pltpu.make_async_remote_copy(
            src_ref=buf.at[slot], dst_ref=buf.at[slot],
            send_sem=send.at[k], recv_sem=recv.at[slot],
            device_id=who, device_id_type=MESH,
        )

    skel_copies = [to_peer(skel_all, skel_send, skel_recv, k, who, m) for k, who in enumerate(peers)]
    for c in skel_copies:
        c.start()
    halo_copies = [
        pltpu.make_async_remote_copy(
            src_ref=halo_out, dst_ref=dst, send_sem=halo_send.at[k], recv_sem=halo_recv.at[k],
            device_id=who, device_id_type=MESH,
        )
        for k, (dst, who) in enumerate([(halo_left, right_id), (halo_right, left_id)])
    ]
    for c in halo_copies:
        c.start()

    src, tgt = features(halo_out[0:ROWS])
    ext_src[block_pts : 2 * block_pts] = src.T.astype(bf16)
    own_tgt[...] = tgt.astype(bf16)
    pad[0:3, 0 : leaf_count * rank] = skel_leaf[...]
    src, tgt = features(pad[:, 0 : leaf_count * rank])
    leaf_src[...] = src.T.astype(bf16)
    leaf_tgt[...] = tgt.astype(bf16)
    _, tgt = features(skel_all[pl.ds(m, 1)][0])
    two_tgt[:, rank:] = tgt.astype(bf16)

    bw = jnp.zeros((vectors, rank), f32)
    for i in range(leaf_count):
        pc = slice(block_pts + i * leaf_size, block_pts + (i + 1) * leaf_size)
        kc = slice(i * rank, (i + 1) * rank)
        lw = apply_kernel(ext_v[leaf_count + i], ext_src[pc], leaf_tgt[:, kc]) * scale(leaf_size)
        bw = bw + apply_kernel(split_rows(lw), leaf_src[kc], two_tgt[:, rank:])
    bw_all[pl.ds(m, 1)] = (bw * scale(leaf_count * rank))[None]
    bw_copies = [to_peer(bw_all, bw_send, bw_recv, k, who, m) for k, who in enumerate(peers)]
    for c in bw_copies:
        c.start()

    for j in range(n_groups):
        pad[0:3, 0:rank] = skel_group[:, j * rank : (j + 1) * rank]
        src, tgt = features(pad[:, 0:rank])
        grp_src[j * rank : (j + 1) * rank] = src.T.astype(bf16)
        pl.when(g == j)(functools.partial(two_tgt.__setitem__, (slice(None), slice(0, rank)), tgt.astype(bf16)))

    for c, buf, base in zip(halo_copies, (halo_left, halo_right), (0, 2 * leaf_count)):
        c.wait_recv()
        src, _ = features(buf[0:ROWS])
        ext_src[base * leaf_size : base * leaf_size + block_pts] = src.T.astype(bf16)
        for i in range(leaf_count):
            ext_v[base + i] = split_rows(buf[ROWS:, i * leaf_size : (i + 1) * leaf_size])

    first_leaf = block * leaf_count - leaf_count
    window = 2 * leaf_count + 1

    def near(i, carry):
        tcol = pl.ds(pl.multiple_of(i * leaf_size, leaf_size), leaf_size)
        target = own_tgt[:, tcol]
        acc = jnp.zeros((vectors, leaf_size), f32)
        for o in range(window):
            e = i + o
            srow = pl.ds(pl.multiple_of(e * leaf_size, leaf_size), leaf_size)
            term = apply_kernel(ext_v[e], ext_src[srow], target)
            if o == leaf_count:
                acc = acc + term
            else:
                times = jnp.int32(0)
                for k in range(slots):
                    hit = (neighbours[i, k] - first_leaf == e) & (k < counts[i])
                    times = times + jnp.where(hit, 1, 0)
                acc = acc + times.astype(f32) * term
        out[:, tcol] = acc * scale(leaf_size)
        return carry

    lax.fori_loop(0, leaf_count // 2, near, 0)

    for j, c in enumerate(peers):
        k = c[1]
        to_peer(skel_all, skel_send, skel_recv, j, c, k).wait_recv()
        to_peer(bw_all, bw_send, bw_recv, j, c, k).wait_recv()

    def from_block(b, carry):
        gw, field = carry
        src, _ = features(skel_all[b])
        r = apply_kernel(split_rows(bw_all[b]), src.T.astype(bf16), two_tgt[...])
        keep = jnp.where(b == m, 0.0, 1.0)
        return gw + r[:, :rank], field + keep * r[:, rank:]

    empty = jnp.zeros((vectors, rank), f32)
    gw, field = lax.fori_loop(0, n_blocks, from_block, (empty, empty))
    field = field * scale((n_blocks - 1) * rank)
    gw_all[pl.ds(g, 1)] = (gw * scale(n_blocks * rank))[None]
    gw_copies = [to_peer(gw_all, gw_send, gw_recv, k, who, g) for k, who in enumerate(cousins)]
    for c in gw_copies:
        c.start()

    lax.fori_loop(leaf_count // 2, leaf_count, near, 0)

    for j, c in enumerate(cousins):
        to_peer(gw_all, gw_send, gw_recv, j, c, c[0]).wait_recv()

    def from_group(h, acc):
        srow = pl.ds(pl.multiple_of(h * rank, rank), rank)
        keep = jnp.where(h == g, 0.0, 1.0)
        return acc + keep * apply_kernel(split_rows(gw_all[h]), grp_src[srow], two_tgt[:, :rank])

    gfield = lax.fori_loop(0, n_groups, from_group, empty) * scale((n_groups - 1) * rank)
    own_rows = pl.ds(pl.multiple_of(g * rank, rank), rank)
    field = field + scale(rank) * apply_kernel(split_rows(gfield), grp_src[own_rows], two_tgt[:, rank:])
    src, _ = features(skel_all[pl.ds(m, 1)][0])
    blk_src[...] = src.T.astype(bf16)
    field2 = split_rows(field)
    for i in range(leaf_count):
        kc = slice(i * rank, (i + 1) * rank)
        pc = slice(i * leaf_size, (i + 1) * leaf_size)
        lf = apply_kernel(field2, blk_src[...], leaf_tgt[:, kc]) * scale(rank)
        out[:, pc] += apply_kernel(split_rows(lf), leaf_src[kc], own_tgt[:, pc]) * scale(rank)

    for c in skel_copies + halo_copies + bw_copies + gw_copies:
        c.wait_send()


def body(n_groups, n_blocks, points, charges, morton, neighbours, counts, skel_leaf, skel_block, skel_group):
    vectors, block_pts = charges.shape
    leaf_count = counts.shape[0]
    leaf_size = block_pts // leaf_count
    rank = skel_block.shape[1]
    slots = neighbours.shape[1]
    vmem = pl.BlockSpec(memory_space=pltpu.VMEM)
    smem = pl.BlockSpec(memory_space=pltpu.SMEM)
    wide = max(block_pts, leaf_count * rank)
    dma = pltpu.SemaphoreType.DMA
    return pl.pallas_call(
        functools.partial(kernel, n_groups, n_blocks, leaf_count, leaf_size, rank, slots),
        out_shape=jax.ShapeDtypeStruct((vectors, block_pts), f32),
        in_specs=[vmem, vmem, vmem, smem, smem, vmem, vmem, vmem],
        out_specs=vmem,
        scratch_shapes=[
            pltpu.VMEM((ROWS, wide), f32),
            pltpu.VMEM((ROWS + vectors, block_pts), f32),
            pltpu.VMEM((ROWS + vectors, block_pts), f32),
            pltpu.VMEM((ROWS + vectors, block_pts), f32),
            pltpu.VMEM((n_blocks, ROWS, rank), f32),
            pltpu.VMEM((n_blocks, vectors, rank), f32),
            pltpu.VMEM((n_groups, vectors, rank), f32),
            pltpu.VMEM((3 * block_pts, FEAT), bf16),
            pltpu.VMEM((3 * leaf_count, 2 * vectors, leaf_size), bf16),
            pltpu.VMEM((FEAT, block_pts), bf16),
            pltpu.VMEM((leaf_count * rank, FEAT), bf16),
            pltpu.VMEM((FEAT, leaf_count * rank), bf16),
            pltpu.VMEM((n_groups * rank, FEAT), bf16),
            pltpu.VMEM((rank, FEAT), bf16),
            pltpu.VMEM((FEAT, 2 * rank), bf16),
            dma((2,)),
            dma((2,)),
            dma((n_blocks - 1,)),
            dma((n_blocks,)),
            dma((n_blocks - 1,)),
            dma((n_blocks,)),
            dma((n_groups - 1,)),
            dma((n_groups,)),
        ],
        compiler_params=pltpu.CompilerParams(
            collective_id=0, has_side_effects=True, vmem_limit_bytes=40 * 1024 * 1024
        ),
    )(points, charges, morton.reshape(1, block_pts), neighbours, counts, skel_leaf, skel_block, skel_group)


def solution(mesh):
    return jax.shard_map(
        functools.partial(body, mesh.shape["grp"], mesh.shape["dev"]),
        mesh=mesh,
        in_specs=(
            P(None, ("grp", "dev")),
            P(None, ("grp", "dev")),
            P(("grp", "dev")),
            P(("grp", "dev"), None),
            P(("grp", "dev")),
            P(None, ("grp", "dev")),
            P(None, ("grp", "dev")),
            P(),
        ),
        out_specs=P(None, ("grp", "dev")),
        check_vma=False,
    )
```

```python
import functools
import math

import jax
import jax.numpy as jnp
from jax import lax
from jax.experimental import pallas as pl
from jax.experimental.pallas import tpu as pltpu
from jax.sharding import PartitionSpec as P

width_sq = 0.1
gain_factor = 5.0
to_base_two = math.sqrt(math.log2(math.e) / width_sq)
middle = 1.0
FEAT = 64
ROWS = 8
MESH = pl.DeviceIdType.MESH
f32, bf16 = jnp.float32, jnp.bfloat16


def parts(x, count):
    out = []
    for _ in range(count - 1):
        out.append(x.astype(bf16).astype(f32))
        x = x - out[-1]
    out.append(x.astype(bf16).astype(f32))
    return out


def features(coords):
    row = lax.broadcasted_iota(jnp.int32, coords.shape, 0)
    c = jnp.where(row < 3, (coords - middle) * to_base_two, 0.0)
    norm = jnp.broadcast_to(jnp.sum(c * c, axis=0, keepdims=True), c.shape)
    hi, mid, lo = parts(c, 3)
    n0, n1, n2 = parts(norm, 3)
    one = jnp.ones_like(c)
    zero = jnp.zeros_like(c)
    first = jnp.where(row == 0, n0, jnp.where(row == 1, n1, n2))
    second = jnp.where(row == 3, n0, jnp.where(row == 4, n1, n2))
    src_n = jnp.where(row < 3, first, jnp.where(row < 6, one, zero))
    tgt_n = jnp.where(row < 3, -one, jnp.where(row < 6, -second, zero))
    hi2, mid2, lo2 = hi + hi, mid + mid, lo + lo
    src = jnp.concatenate([hi, hi, mid, mid, hi, lo, src_n, zero], axis=0)
    tgt = jnp.concatenate([hi2, mid2, hi2, mid2, lo2, hi2, tgt_n, zero], axis=0)
    return src, tgt


def split_rows(v):
    return jnp.concatenate(parts(v, 2), axis=0).astype(bf16)


CHUNK = 64


def fill_kernel(src, tgt, k_hi, k_lo, row, col):
    for r in range(0, src.shape[0], CHUNK):
        k = jnp.exp2(jnp.dot(src[r : r + CHUNK], tgt, preferred_element_type=f32))
        hi = k.astype(bf16)
        at = (slice(row + r, row + r + CHUNK), slice(col, col + tgt.shape[1]))
        k_hi[at] = hi
        k_lo[at] = (k - hi.astype(f32)).astype(bf16)


def times_kernel(v2, k_hi, k_lo, contract=0):
    half = v2.shape[0] // 2
    dims = (((1,), (contract,)), ((), ()))
    r = lax.dot_general(v2, k_hi, dims, preferred_element_type=f32)
    q = lax.dot_general(v2[:half], k_lo, dims, preferred_element_type=f32)
    return r[:half] + r[half:] + q


def repeat(number, step):
    if number <= 8:
        for index in range(number):
            step(index)
    else:
        lax.fori_loop(0, number, lambda index, carry: (step(index), carry)[1], 0)


def kernel(
    n_groups, n_blocks, leaf_count, leaf_size, rank, slots,
    points_in, charges_in, morton_in, neighbours_in, counts_in, skel_leaf_in, skel_block_in, skel_group_in,
    out,
    points, charges, morton, neighbours, counts, skel_leaf, skel_block, skel_group,
    pad_pts, pad_leaf, pad_grp, halo_out, halo_left, halo_right, skel_all, bw_all, gw_all,
    ext_src, ext_c, own_tgt, leaf_src, leaf_tgt, two_tgt,
    kp_hi, kp_lo, kl_hi, kl_lo, kb_hi, kb_lo, kg_hi, kg_lo, kn_hi, kn_lo,
    in_sem, halo_send, halo_recv, skel_send, skel_recv, bw_send, bw_recv, gw_send, gw_recv,
):
    vectors, block_pts = charges.shape
    g = lax.axis_index("grp")
    m = lax.axis_index("dev")
    block = g * n_blocks + m
    total = n_groups * n_blocks
    right = lax.rem(block + 1, total)
    left = lax.rem(block + total - 1, total)
    right_id = (right // n_blocks, lax.rem(right, n_blocks))
    left_id = (left // n_blocks, lax.rem(left, n_blocks))
    peers = [(g, lax.rem(m + d, n_blocks)) for d in range(1, n_blocks)]
    cousins = [(lax.rem(g + d, n_groups), m) for d in range(1, n_groups)]

    barrier = pltpu.get_barrier_semaphore()
    greeted = [left_id, right_id] + peers + cousins
    for who in greeted:
        pl.semaphore_signal(barrier, inc=1, device_id=who, device_id_type=MESH)

    pairs = [
        (skel_block_in, skel_block), (skel_leaf_in, skel_leaf), (morton_in, morton), (points_in, points),
        (charges_in, charges), (skel_group_in, skel_group), (neighbours_in, neighbours), (counts_in, counts),
    ]
    loads = [pltpu.make_async_copy(a, b, in_sem.at[k]) for k, (a, b) in enumerate(pairs)]
    for c in loads:
        c.start()

    def scale(terms):
        return gain_factor / math.sqrt(terms)

    for p in (pad_pts, pad_leaf, pad_grp):
        p[...] = jnp.zeros_like(p)
    skel_all[pl.ds(m, 1)] = jnp.zeros((1, ROWS, rank), f32)

    loads[0].wait()
    skel_all[pl.ds(m, 1), 0:3] = skel_block[...][None]
    loads[1].wait()
    pad_leaf[0:3] = skel_leaf[...]
    _, tgt = features(skel_all[pl.ds(m, 1)][0])
    two_tgt[:, rank:] = tgt.astype(bf16)
    src, tgt = features(pad_leaf[...])
    leaf_src[...] = src.T.astype(bf16)
    leaf_tgt[...] = tgt.astype(bf16)
    fill_kernel(leaf_src[...], two_tgt[:, rank:], kl_hi, kl_lo, 0, 0)

    for c in loads[2:5]:
        c.wait()
    pad_pts[0:3] = points[...]
    pts = pad_pts[...]
    stacked = jnp.concatenate(
        parts(pts, 3) + [jnp.zeros_like(pts)] + parts(charges[...], 2), axis=0
    ).astype(bf16)
    place = lax.broadcasted_iota(jnp.int32, (leaf_size, leaf_size), 0)
    for i in range(leaf_count):
        cols = slice(i * leaf_size, (i + 1) * leaf_size)
        s = jnp.zeros((stacked.shape[0], leaf_size), f32)
        for r in range(0, block_pts, leaf_size):
            onehot = jnp.where(place == morton[0:1, cols] - r, 1.0, 0.0).astype(bf16)
            s = s + jnp.dot(stacked[:, r : r + leaf_size], onehot, preferred_element_type=f32)
        halo_out[0:ROWS, cols] = s[0:8] + s[8:16] + s[16:24]
        halo_out[ROWS:, cols] = s[32 : 32 + vectors] + s[32 + vectors :]

    pl.semaphore_wait(barrier, len(greeted))

    def to_peer(buf, send, recv, k, who, slot):
        return pltpu.make_async_remote_copy(
            src_ref=buf.at[slot], dst_ref=buf.at[slot],
            send_sem=send.at[k], recv_sem=recv.at[slot],
            device_id=who, device_id_type=MESH,
        )

    skel_copies = [to_peer(skel_all, skel_send, skel_recv, k, who, m) for k, who in enumerate(peers)]
    for c in skel_copies:
        c.start()
    halo_copies = [
        pltpu.make_async_remote_copy(
            src_ref=halo_out, dst_ref=dst, send_sem=halo_send.at[k], recv_sem=halo_recv.at[k],
            device_id=who, device_id_type=MESH,
        )
        for k, (dst, who) in enumerate([(halo_left, right_id), (halo_right, left_id)])
    ]
    for c in halo_copies:
        c.start()

    src, tgt = features(halo_out[0:ROWS])
    ext_src[block_pts : 2 * block_pts] = src.T.astype(bf16)
    own_tgt[...] = tgt.astype(bf16)
    ext_c[:, block_pts : 2 * block_pts] = halo_out[ROWS:]
    leaf_w = []
    for i in range(leaf_count):
        pc = slice(i * leaf_size, (i + 1) * leaf_size)
        kc = slice(i * rank, (i + 1) * rank)
        fill_kernel(ext_src[block_pts + i * leaf_size : block_pts + (i + 1) * leaf_size], leaf_tgt[:, kc], kp_hi, kp_lo, i * leaf_size, 0)
        leaf_w.append(times_kernel(split_rows(halo_out[ROWS:, pc]), kp_hi[pc], kp_lo[pc]) * scale(leaf_size))
    lw = jnp.concatenate(leaf_w, axis=1)
    bw_all[pl.ds(m, 1)] = (times_kernel(split_rows(lw), kl_hi[...], kl_lo[...]) * scale(leaf_count * rank))[None]
    bw_copies = [to_peer(bw_all, bw_send, bw_recv, k, who, m) for k, who in enumerate(peers)]
    for c in bw_copies:
        c.start()

    loads[5].wait()
    pad_grp[0:3] = skel_group[...]
    src, tgt = features(pad_grp[...])
    grp_src = src.T.astype(bf16)
    for j in range(n_groups):
        pl.when(g == j)(functools.partial(
            two_tgt.__setitem__, (slice(None), slice(0, rank)), tgt[:, j * rank : (j + 1) * rank].astype(bf16)))
    for j, c in enumerate(peers):
        to_peer(skel_all, skel_send, skel_recv, j, c, c[1]).wait_recv()

    def from_block(b):
        src, _ = features(skel_all[b])
        fill_kernel(src.T.astype(bf16), two_tgt[...], kb_hi.at[b], kb_lo.at[b], 0, 0)

    repeat(n_blocks, from_block)

    for j, c in enumerate(peers):
        to_peer(bw_all, bw_send, bw_recv, j, c, c[1]).wait_recv()

    def add_block(b, carry):
        gw, field = carry
        r = times_kernel(split_rows(bw_all[b]), kb_hi[b], kb_lo[b])
        keep = jnp.where(b == m, 0.0, 1.0)
        return gw + r[:, :rank], field + keep * r[:, rank:]

    empty = jnp.zeros((vectors, rank), f32)
    gw, field = lax.fori_loop(0, n_blocks, add_block, (empty, empty), unroll=True if n_blocks <= 8 else 1)
    field = field * scale((n_blocks - 1) * rank)
    gw_all[pl.ds(g, 1)] = (gw * scale(n_blocks * rank))[None]
    gw_copies = [to_peer(gw_all, gw_send, gw_recv, k, who, g) for k, who in enumerate(cousins)]
    for c in gw_copies:
        c.start()

    fill_kernel(grp_src, two_tgt[:, :rank], kg_hi, kg_lo, 0, 0)

    for c, buf, base in zip(halo_copies, (halo_left, halo_right), (0, 2 * block_pts)):
        c.wait_recv()
        src, _ = features(buf[0:ROWS])
        ext_src[base : base + block_pts] = src.T.astype(bf16)
        ext_c[:, base : base + block_pts] = buf[ROWS:]
    loads[6].wait()
    loads[7].wait()
    first_leaf = block * leaf_count - leaf_count
    window = 2 * leaf_count + 1
    near = []
    for i in range(leaf_count):
        span = slice(i * leaf_size, (i + window) * leaf_size)
        fill_kernel(ext_src[span], own_tgt[:, i * leaf_size : (i + 1) * leaf_size], kn_hi.at[i], kn_lo.at[i], 0, 0)
        values = []
        for o in range(window):
            e = i + o
            piece = ext_c[:, e * leaf_size : (e + 1) * leaf_size]
            if o != leaf_count:
                times = jnp.int32(0)
                for k in range(slots):
                    hit = (neighbours[i, k] - first_leaf == e) & (k < counts[i])
                    times = times + jnp.where(hit, 1, 0)
                piece = piece * times.astype(f32)
            values.append(piece)
        near.append(times_kernel(split_rows(jnp.concatenate(values, axis=1)), kn_hi[i], kn_lo[i]))

    for j, c in enumerate(cousins):
        to_peer(gw_all, gw_send, gw_recv, j, c, c[0]).wait_recv()

    def add_group(h, acc):
        rows = pl.ds(pl.multiple_of(h * rank, rank), rank)
        keep = jnp.where(h == g, 0.0, 1.0)
        return acc + keep * times_kernel(split_rows(gw_all[h]), kg_hi[rows], kg_lo[rows])

    gfield = lax.fori_loop(0, n_groups, add_group, empty, unroll=True if n_groups <= 8 else 1)
    gfield = gfield * scale((n_groups - 1) * rank)
    down_hi = kb_hi[pl.ds(m, 1), :, 0:rank][0]
    down_lo = kb_lo[pl.ds(m, 1), :, 0:rank][0]
    field = field + scale(rank) * times_kernel(split_rows(gfield), down_hi, down_lo, 1)
    lf = times_kernel(split_rows(field), kl_hi[...], kl_lo[...], 1) * scale(rank)
    for i in range(leaf_count):
        pc = slice(i * leaf_size, (i + 1) * leaf_size)
        far = times_kernel(split_rows(lf[:, i * rank : (i + 1) * rank]), kp_hi[pc], kp_lo[pc], 1)
        out[:, pc] = near[i] * scale(leaf_size) + far * scale(rank)

    for c in skel_copies + halo_copies + bw_copies + gw_copies:
        c.wait_send()


def body(n_groups, n_blocks, points, charges, morton, neighbours, counts, skel_leaf, skel_block, skel_group):
    vectors, block_pts = charges.shape
    leaf_count = counts.shape[0]
    leaf_size = block_pts // leaf_count
    rank = skel_block.shape[1]
    slots = neighbours.shape[1]
    leaf_cols = leaf_count * rank
    window = (2 * leaf_count + 1) * leaf_size
    dma = pltpu.SemaphoreType.DMA
    morton = morton.reshape(1, block_pts)
    operands = (points, charges, morton, neighbours, counts, skel_leaf, skel_block, skel_group)
    places = (pltpu.VMEM,) * 3 + (pltpu.SMEM,) * 2 + (pltpu.VMEM,) * 3
    both = lambda *shape: [pltpu.VMEM(shape, bf16)] * 2
    return pl.pallas_call(
        functools.partial(kernel, n_groups, n_blocks, leaf_count, leaf_size, rank, slots),
        out_shape=jax.ShapeDtypeStruct((vectors, block_pts), f32),
        in_specs=[pl.BlockSpec(memory_space=pltpu.HBM)] * len(operands),
        out_specs=pl.BlockSpec(memory_space=pltpu.VMEM),
        scratch_shapes=[
            *[place(a.shape, a.dtype) for place, a in zip(places, operands)],
            pltpu.VMEM((ROWS, block_pts), f32),
            pltpu.VMEM((ROWS, leaf_cols), f32),
            pltpu.VMEM((ROWS, n_groups * rank), f32),
            pltpu.VMEM((ROWS + vectors, block_pts), f32),
            pltpu.VMEM((ROWS + vectors, block_pts), f32),
            pltpu.VMEM((ROWS + vectors, block_pts), f32),
            pltpu.VMEM((n_blocks, ROWS, rank), f32),
            pltpu.VMEM((n_blocks, vectors, rank), f32),
            pltpu.VMEM((n_groups, vectors, rank), f32),
            pltpu.VMEM((3 * block_pts, FEAT), bf16),
            pltpu.VMEM((vectors, 3 * block_pts), f32),
            pltpu.VMEM((FEAT, block_pts), bf16),
            pltpu.VMEM((leaf_cols, FEAT), bf16),
            pltpu.VMEM((FEAT, leaf_cols), bf16),
            pltpu.VMEM((FEAT, 2 * rank), bf16),
            *both(block_pts, rank),
            *both(leaf_cols, rank),
            *both(n_blocks, rank, 2 * rank),
            *both(n_groups * rank, rank),
            *both(leaf_count, window, leaf_size),
            dma((len(operands),)),
            dma((2,)),
            dma((2,)),
            dma((n_blocks - 1,)),
            dma((n_blocks,)),
            dma((n_blocks - 1,)),
            dma((n_blocks,)),
            dma((n_groups - 1,)),
            dma((n_groups,)),
        ],
        compiler_params=pltpu.CompilerParams(
            collective_id=0, has_side_effects=True, vmem_limit_bytes=48 * 1024 * 1024
        ),
    )(*operands)


def solution(mesh):
    return jax.shard_map(
        functools.partial(body, mesh.shape["grp"], mesh.shape["dev"]),
        mesh=mesh,
        in_specs=(
            P(None, ("grp", "dev")),
            P(None, ("grp", "dev")),
            P(("grp", "dev")),
            P(("grp", "dev"), None),
            P(("grp", "dev")),
            P(None, ("grp", "dev")),
            P(None, ("grp", "dev")),
            P(),
        ),
        out_specs=P(None, ("grp", "dev")),
        check_vma=False,
    )
```

```python
import functools
import math

import jax
import jax.numpy as jnp
from jax import lax
from jax.experimental import pallas as pl
from jax.experimental.pallas import tpu as pltpu
from jax.sharding import PartitionSpec as P

width_sq = 0.1
gain_factor = 5.0
to_base_two = math.sqrt(math.log2(math.e) / width_sq)
middle = 1.0
FEAT = 64
ROWS = 8
MESH = pl.DeviceIdType.MESH
f32, bf16 = jnp.float32, jnp.bfloat16


def parts(x, count):
    out = []
    for _ in range(count - 1):
        out.append(x.astype(bf16).astype(f32))
        x = x - out[-1]
    out.append(x.astype(bf16).astype(f32))
    return out


def features(coords):
    row = lax.broadcasted_iota(jnp.int32, coords.shape, 0)
    c = jnp.where(row < 3, (coords - middle) * to_base_two, 0.0)
    norm = jnp.broadcast_to(jnp.sum(c * c, axis=0, keepdims=True), c.shape)
    hi, mid, lo = parts(c, 3)
    n0, n1, n2 = parts(norm, 3)
    one = jnp.ones_like(c)
    zero = jnp.zeros_like(c)
    first = jnp.where(row == 0, n0, jnp.where(row == 1, n1, n2))
    second = jnp.where(row == 3, n0, jnp.where(row == 4, n1, n2))
    src_n = jnp.where(row < 3, first, jnp.where(row < 6, one, zero))
    tgt_n = jnp.where(row < 3, -one, jnp.where(row < 6, -second, zero))
    hi2, mid2, lo2 = hi + hi, mid + mid, lo + lo
    src = jnp.concatenate([hi, hi, mid, mid, hi, lo, src_n, zero], axis=0)
    tgt = jnp.concatenate([hi2, mid2, hi2, mid2, lo2, hi2, tgt_n, zero], axis=0)
    return src, tgt


def split_rows(v):
    return jnp.concatenate(parts(v, 2), axis=0).astype(bf16)


CHUNK = 64


def fill_kernel(src, tgt, k_hi, k_lo, row, col):
    for r in range(0, src.shape[0], CHUNK):
        k = jnp.exp2(jnp.dot(src[r : r + CHUNK], tgt, preferred_element_type=f32))
        hi = k.astype(bf16)
        at = (slice(row + r, row + r + CHUNK), slice(col, col + tgt.shape[1]))
        k_hi[at] = hi
        k_lo[at] = (k - hi.astype(f32)).astype(bf16)


def times_kernel(v2, k_hi, k_lo, contract=0):
    half = v2.shape[0] // 2
    dims = (((1,), (contract,)), ((), ()))
    r = lax.dot_general(v2, k_hi, dims, preferred_element_type=f32)
    q = lax.dot_general(v2[:half], k_lo, dims, preferred_element_type=f32)
    return r[:half] + r[half:] + q


def repeat(number, step):
    if number <= 8:
        for index in range(1, number):
            step(index)
    else:
        lax.fori_loop(1, number, lambda index, carry: (step(index), carry)[1], 0)


def gather_terms(number, step, start):
    if number <= 8:
        for index in range(1, number):
            start = step(index, start)
        return start
    return lax.fori_loop(1, number, step, start)


def kernel(
    n_groups, n_blocks, leaf_count, leaf_size, rank, slots,
    points_in, charges_in, morton_in, neighbours_in, counts_in, skel_leaf_in, skel_block_in, skel_group_in,
    out,
    points, charges, morton, neighbours, counts, skel_leaf, skel_block, skel_group,
    pad_pts, pad_leaf, pad_grp, halo_out, halo_left, halo_right, msg, gw_all,
    ext_src, ext_c, own_tgt, leaf_src, leaf_tgt, grp_src, grp_tgt, blk_tgt,
    kp_hi, kp_lo, kl_hi, kl_lo, kr_hi, kr_lo, kb_hi, kb_lo, kg_hi, kg_lo, kn_hi, kn_lo,
    in_sem, halo_send, halo_recv, msg_send, msg_recv, gw_send, gw_recv,
):
    vectors, block_pts = charges.shape
    g = lax.axis_index("grp")
    m = lax.axis_index("dev")
    block = g * n_blocks + m
    total = n_groups * n_blocks
    right = lax.rem(block + 1, total)
    left = lax.rem(block + total - 1, total)
    right_id = (right // n_blocks, lax.rem(right, n_blocks))
    left_id = (left // n_blocks, lax.rem(left, n_blocks))
    peers = [(g, lax.rem(m + d, n_blocks)) for d in range(1, n_blocks)]
    cousins = [(lax.rem(g + d, n_groups), m) for d in range(1, n_groups)]

    barrier = pltpu.get_barrier_semaphore()
    greeted = [left_id, right_id] + peers + cousins
    for who in greeted:
        pl.semaphore_signal(barrier, inc=1, device_id=who, device_id_type=MESH)

    pairs = [
        (skel_block_in, skel_block), (skel_leaf_in, skel_leaf), (skel_group_in, skel_group), (morton_in, morton),
        (points_in, points), (charges_in, charges), (neighbours_in, neighbours), (counts_in, counts),
    ]
    loads = [pltpu.make_async_copy(a, b, in_sem.at[k]) for k, (a, b) in enumerate(pairs)]
    for c in loads:
        c.start()

    def scale(terms):
        return gain_factor / math.sqrt(terms)

    def leaf_cols(i):
        return slice(i * leaf_size, (i + 1) * leaf_size)

    def rank_cols(i):
        return slice(i * rank, (i + 1) * rank)

    for p in (pad_pts, pad_leaf, pad_grp):
        p[...] = jnp.zeros_like(p)
    own = pl.ds(m, 1)
    bw_rows = slice(ROWS, ROWS + vectors)
    up_rows = slice(ROWS + vectors, ROWS + 2 * vectors)
    msg[own, 0:ROWS] = jnp.zeros((1, ROWS, rank), f32)

    loads[0].wait()
    msg[own, 0:3] = skel_block[...][None]
    loads[1].wait()
    pad_leaf[0:3] = skel_leaf[...]
    src_b, tgt = features(msg[own, 0:ROWS][0])
    blk_tgt[...] = tgt.astype(bf16)
    src, tgt = features(pad_leaf[...])
    leaf_src[...] = src.T.astype(bf16)
    leaf_tgt[...] = tgt.astype(bf16)
    fill_kernel(leaf_src[...], blk_tgt[...], kl_hi, kl_lo, 0, 0)
    loads[2].wait()
    pad_grp[0:3] = skel_group[...]
    src, tgt = features(pad_grp[...])
    grp_src[...] = src.T.astype(bf16)
    for j in range(n_groups):
        pl.when(g == j)(functools.partial(
            grp_tgt.__setitem__, (slice(None), slice(None)), tgt[:, rank_cols(j)].astype(bf16)))
    fill_kernel(src_b.T.astype(bf16), grp_tgt[...], kr_hi, kr_lo, 0, 0)

    for c in loads[3:6]:
        c.wait()
    pad_pts[0:3] = points[...]
    pts = pad_pts[...]
    stacked = jnp.concatenate(
        parts(pts, 3) + [jnp.zeros_like(pts)] + parts(charges[...], 2), axis=0
    ).astype(bf16)
    place = lax.broadcasted_iota(jnp.int32, (leaf_size, leaf_size), 0)
    for i in range(leaf_count):
        s = jnp.zeros((stacked.shape[0], leaf_size), f32)
        for r in range(0, block_pts, leaf_size):
            onehot = jnp.where(place == morton[0:1, leaf_cols(i)] - r, 1.0, 0.0).astype(bf16)
            s = s + jnp.dot(stacked[:, r : r + leaf_size], onehot, preferred_element_type=f32)
        halo_out[0:ROWS, leaf_cols(i)] = s[0:8] + s[8:16] + s[16:24]
        halo_out[ROWS:, leaf_cols(i)] = s[32 : 32 + vectors] + s[32 + vectors :]

    src, tgt = features(halo_out[0:ROWS])
    ext_src[block_pts : 2 * block_pts] = src.T.astype(bf16)
    own_tgt[...] = tgt.astype(bf16)
    leaf_w = []
    for i in range(leaf_count):
        fill_kernel(ext_src[leaf_cols(leaf_count + i)], leaf_tgt[:, rank_cols(i)], kp_hi, kp_lo, i * leaf_size, 0)
        leaf_w.append(times_kernel(split_rows(halo_out[ROWS:, leaf_cols(i)]), kp_hi[leaf_cols(i)], kp_lo[leaf_cols(i)]))
    lw = jnp.concatenate(leaf_w, axis=1) * scale(leaf_size)
    bw = times_kernel(split_rows(lw), kl_hi[...], kl_lo[...]) * scale(leaf_count * rank)
    msg[own, bw_rows] = bw[None]
    msg[own, up_rows] = (times_kernel(split_rows(bw), kr_hi[...], kr_lo[...]) * scale(n_blocks * rank))[None]

    pl.semaphore_wait(barrier, len(greeted))

    def to_peer(buf, send, recv, k, who, slot):
        return pltpu.make_async_remote_copy(
            src_ref=buf.at[slot], dst_ref=buf.at[slot],
            send_sem=send.at[k], recv_sem=recv.at[slot],
            device_id=who, device_id_type=MESH,
        )

    msg_copies = [to_peer(msg, msg_send, msg_recv, k, who, m) for k, who in enumerate(peers)]
    halo_copies = [
        pltpu.make_async_remote_copy(
            src_ref=halo_out, dst_ref=dst, send_sem=halo_send.at[k], recv_sem=halo_recv.at[k],
            device_id=who, device_id_type=MESH,
        )
        for k, (dst, who) in enumerate([(halo_left, right_id), (halo_right, left_id)])
    ]
    for c in msg_copies + halo_copies:
        c.start()

    ext_c[:, block_pts : 2 * block_pts] = halo_out[ROWS:]
    loads[6].wait()
    loads[7].wait()
    first_leaf = block * leaf_count - leaf_count

    def values(i, e):
        piece = ext_c[:, leaf_cols(e)]
        if e == leaf_count + i:
            return piece
        times = jnp.int32(0)
        for k in range(slots):
            hit = (neighbours[i, k] - first_leaf == e) & (k < counts[i])
            times = times + jnp.where(hit, 1, 0)
        return piece * times.astype(f32)

    def joined(pieces):
        return split_rows(jnp.concatenate(pieces, axis=1))

    near = []
    for i in range(leaf_count):
        rows = (i + 1) * leaf_size
        fill_kernel(
            ext_src[block_pts : block_pts + rows], own_tgt[:, leaf_cols(i)], kn_hi.at[i], kn_lo.at[i], 0, 0)
    for i in range(leaf_count):
        rows = (i + 1) * leaf_size
        v2 = joined([values(i, leaf_count + j) for j in range(i + 1)])
        acc = times_kernel(v2, kn_hi[i, 0:rows], kn_lo[i, 0:rows])
        for j in range(i + 1, leaf_count):
            acc = acc + times_kernel(
                split_rows(values(i, leaf_count + j)), kn_hi[j, leaf_cols(i)], kn_lo[j, leaf_cols(i)], 1)
        near.append(acc)

    for j, c in enumerate(peers):
        to_peer(msg, msg_send, msg_recv, j, c, c[1]).wait_recv()
    gw_all[pl.ds(g, 1)] = jnp.sum(msg[:, up_rows], axis=0, keepdims=True)
    gw_copies = [to_peer(gw_all, gw_send, gw_recv, k, who, g) for k, who in enumerate(cousins)]
    for c in gw_copies:
        c.start()

    empty = jnp.zeros((vectors, rank), f32)

    def cousin_rows(d):
        return pl.ds(pl.multiple_of(lax.rem(g + d, n_groups) * rank, rank), rank)

    def fill_group(d):
        fill_kernel(grp_src[cousin_rows(d)], grp_tgt[...], kg_hi.at[d - 1], kg_lo.at[d - 1], 0, 0)

    def fill_peer(d):
        src, _ = features(msg[lax.rem(m + d, n_blocks), 0:ROWS])
        fill_kernel(src.T.astype(bf16), blk_tgt[...], kb_hi.at[d - 1], kb_lo.at[d - 1], 0, 0)

    def add_peer(d, acc):
        v2 = split_rows(msg[lax.rem(m + d, n_blocks), bw_rows])
        return acc + times_kernel(v2, kb_hi[d - 1], kb_lo[d - 1])

    repeat(n_groups, fill_group)
    repeat(n_blocks, fill_peer)
    field = gather_terms(n_blocks, add_peer, empty) * scale((n_blocks - 1) * rank)

    for c, buf, base in zip(halo_copies, (halo_left, halo_right), (0, 2 * block_pts)):
        c.wait_recv()
        src, _ = features(buf[0:ROWS])
        ext_src[base : base + block_pts] = src.T.astype(bf16)
        ext_c[:, base : base + block_pts] = buf[ROWS:]
    for i in range(leaf_count):
        base = leaf_count * leaf_size
        before = list(range(i, leaf_count))
        after = list(range(2 * leaf_count, 2 * leaf_count + i + 1))
        split = base + len(before) * leaf_size
        end = split + len(after) * leaf_size
        target = own_tgt[:, leaf_cols(i)]
        fill_kernel(ext_src[i * leaf_size : block_pts], target, kn_hi.at[i], kn_lo.at[i], base, 0)
        fill_kernel(
            ext_src[2 * block_pts : 2 * block_pts + len(after) * leaf_size], target, kn_hi.at[i], kn_lo.at[i], split, 0)
        v2 = joined([values(i, e) for e in before + after])
        near[i] = near[i] + times_kernel(v2, kn_hi[i, base:end], kn_lo[i, base:end])

    for j, c in enumerate(cousins):
        to_peer(gw_all, gw_send, gw_recv, j, c, c[0]).wait_recv()

    def add_group(d, acc):
        v2 = split_rows(gw_all[lax.rem(g + d, n_groups)])
        return acc + times_kernel(v2, kg_hi[d - 1], kg_lo[d - 1])

    gfield = gather_terms(n_groups, add_group, empty) * scale((n_groups - 1) * rank)
    field = field + scale(rank) * times_kernel(split_rows(gfield), kr_hi[...], kr_lo[...], 1)
    lf = times_kernel(split_rows(field), kl_hi[...], kl_lo[...], 1) * scale(rank)
    for i in range(leaf_count):
        far = times_kernel(split_rows(lf[:, rank_cols(i)]), kp_hi[leaf_cols(i)], kp_lo[leaf_cols(i)], 1)
        out[:, leaf_cols(i)] = near[i] * scale(leaf_size) + far * scale(rank)

    for c in msg_copies + halo_copies + gw_copies:
        c.wait_send()


def body(n_groups, n_blocks, points, charges, morton, neighbours, counts, skel_leaf, skel_block, skel_group):
    vectors, block_pts = charges.shape
    leaf_count = counts.shape[0]
    leaf_size = block_pts // leaf_count
    rank = skel_block.shape[1]
    slots = neighbours.shape[1]
    leaf_cols = leaf_count * rank
    window = (2 * leaf_count + 1) * leaf_size
    dma = pltpu.SemaphoreType.DMA
    morton = morton.reshape(1, block_pts)
    operands = (points, charges, morton, neighbours, counts, skel_leaf, skel_block, skel_group)
    places = (pltpu.VMEM,) * 3 + (pltpu.SMEM,) * 2 + (pltpu.VMEM,) * 3
    both = lambda *shape: [pltpu.VMEM(shape, bf16)] * 2
    return pl.pallas_call(
        functools.partial(kernel, n_groups, n_blocks, leaf_count, leaf_size, rank, slots),
        out_shape=jax.ShapeDtypeStruct((vectors, block_pts), f32),
        in_specs=[pl.BlockSpec(memory_space=pltpu.HBM)] * len(operands),
        out_specs=pl.BlockSpec(memory_space=pltpu.VMEM),
        scratch_shapes=[
            *[place(a.shape, a.dtype) for place, a in zip(places, operands)],
            pltpu.VMEM((ROWS, block_pts), f32),
            pltpu.VMEM((ROWS, leaf_cols), f32),
            pltpu.VMEM((ROWS, n_groups * rank), f32),
            pltpu.VMEM((ROWS + vectors, block_pts), f32),
            pltpu.VMEM((ROWS + vectors, block_pts), f32),
            pltpu.VMEM((ROWS + vectors, block_pts), f32),
            pltpu.VMEM((n_blocks, ROWS + 2 * vectors, rank), f32),
            pltpu.VMEM((n_groups, vectors, rank), f32),
            pltpu.VMEM((3 * block_pts, FEAT), bf16),
            pltpu.VMEM((vectors, 3 * block_pts), f32),
            pltpu.VMEM((FEAT, block_pts), bf16),
            pltpu.VMEM((leaf_cols, FEAT), bf16),
            pltpu.VMEM((FEAT, leaf_cols), bf16),
            pltpu.VMEM((n_groups * rank, FEAT), bf16),
            pltpu.VMEM((FEAT, rank), bf16),
            pltpu.VMEM((FEAT, rank), bf16),
            *both(block_pts, rank),
            *both(leaf_cols, rank),
            *both(rank, rank),
            *both(n_blocks - 1, rank, rank),
            *both(n_groups - 1, rank, rank),
            *both(leaf_count, window, leaf_size),
            dma((len(operands),)),
            dma((2,)),
            dma((2,)),
            dma((n_blocks - 1,)),
            dma((n_blocks,)),
            dma((n_groups - 1,)),
            dma((n_groups,)),
        ],
        compiler_params=pltpu.CompilerParams(
            collective_id=0, has_side_effects=True, vmem_limit_bytes=64 * 1024 * 1024
        ),
    )(*operands)


def solution(mesh):
    return jax.shard_map(
        functools.partial(body, mesh.shape["grp"], mesh.shape["dev"]),
        mesh=mesh,
        in_specs=(
            P(None, ("grp", "dev")),
            P(None, ("grp", "dev")),
            P(("grp", "dev")),
            P(("grp", "dev"), None),
            P(("grp", "dev")),
            P(None, ("grp", "dev")),
            P(None, ("grp", "dev")),
            P(),
        ),
        out_specs=P(None, ("grp", "dev")),
        check_vma=False,
    )
```

```python
import functools
import math

import jax
import jax.numpy as jnp
from jax import lax
from jax.experimental import pallas as pl
from jax.experimental.pallas import tpu as pltpu
from jax.sharding import PartitionSpec as P

width_sq = 0.1
gain_factor = 5.0
to_base_two = math.sqrt(math.log2(math.e) / width_sq)
middle = 1.0
FEAT = 32
ROWS = 8
SENT = 4
MESH = pl.DeviceIdType.MESH
f32, bf16 = jnp.float32, jnp.bfloat16


def parts(x, count):
    out = []
    for _ in range(count - 1):
        out.append(x.astype(bf16).astype(f32))
        x = x - out[-1]
    out.append(x.astype(bf16).astype(f32))
    return out


def features(coords):
    row = lax.broadcasted_iota(jnp.int32, coords.shape, 0)
    low, used = row < 3, row < 6
    c = jnp.where(used, (coords - middle) * to_base_two, 0.0)
    norm = jnp.sum(jnp.where(low, c * c, 0.0), axis=0, keepdims=True)
    norm = jnp.broadcast_to(norm, c.shape)
    hi, mid, lo = parts(c, 3)
    n0, n1, n2 = parts(norm, 3)
    nth = jnp.where((row == 0) | (row == 3), n0, jnp.where((row == 1) | (row == 4), n1, n2))
    src_n = jnp.where(low, nth, jnp.where(used, 1.0, 0.0))
    tgt_n = jnp.where(low, -1.0, jnp.where(used, -nth, 0.0))
    upper = jnp.where(low, hi + hi, mid + mid)
    src = jnp.concatenate([hi, mid, jnp.where(low, hi, lo), src_n], axis=0)
    tgt = jnp.concatenate([upper, upper, jnp.where(low, lo + lo, hi + hi), tgt_n], axis=0)
    return src, tgt


def split_rows(v):
    return jnp.concatenate(parts(v, 2), axis=0).astype(bf16)


CHUNK = 64


def fill_kernel(src, tgt, k_hi, k_lo, row, col):
    for r in range(0, src.shape[0], CHUNK):
        k = jnp.exp2(jnp.dot(src[r : r + CHUNK], tgt, preferred_element_type=f32))
        hi = k.astype(bf16)
        at = (slice(row + r, row + r + CHUNK), slice(col, col + tgt.shape[1]))
        k_hi[at] = hi
        k_lo[at] = (k - hi.astype(f32)).astype(bf16)


def times_kernel(v2, k_hi, k_lo, contract=0):
    half = v2.shape[0] // 2
    dims = (((1,), (contract,)), ((), ()))
    r = lax.dot_general(v2, k_hi, dims, preferred_element_type=f32)
    q = lax.dot_general(v2[:half], k_lo, dims, preferred_element_type=f32)
    return r[:half] + r[half:] + q


def repeat(number, step):
    if number <= 8:
        for index in range(1, number):
            step(index)
    else:
        lax.fori_loop(1, number, lambda index, carry: (step(index), carry)[1], 0)


def gather_terms(number, step, start):
    if number <= 8:
        for index in range(1, number):
            start = step(index, start)
        return start
    return lax.fori_loop(1, number, step, start)


def kernel(
    n_groups, n_blocks, leaf_count, leaf_size, rank, slots,
    points_in, charges_in, morton_in, neighbours_in, counts_in, skel_leaf_in, skel_block_in, skel_group_in,
    out,
    points, charges, morton, neighbours, counts, skel_leaf, skel_block, skel_group,
    pad_pts, pad_leaf, pad_grp, pad_blk, pad_left, pad_right, sorted_pts, chg_out, chg_left, chg_right,
    pts_out, pts_left, pts_right, skel_all, up_out, up_in, bw_all, gw_out, gw_all,
    ext_src, ext_c, own_tgt, leaf_src, leaf_tgt, grp_src, grp_tgt, blk_tgt,
    kp_hi, kp_lo, kl_hi, kl_lo, kr_hi, kr_lo, kb_hi, kb_lo, kg_hi, kg_lo, kn_hi, kn_lo,
    in_sem, halo_send, halo_recv, skel_send, skel_recv, up_send, up_recv, bw_send, bw_recv, gw_send, gw_recv,
):
    vectors, block_pts = charges.shape
    g = lax.axis_index("grp")
    m = lax.axis_index("dev")
    block = g * n_blocks + m
    total = n_groups * n_blocks
    right = lax.rem(block + 1, total)
    left = lax.rem(block + total - 1, total)
    right_id = (right // n_blocks, lax.rem(right, n_blocks))
    left_id = (left // n_blocks, lax.rem(left, n_blocks))
    peers = [(g, lax.rem(m + d, n_blocks)) for d in range(1, n_blocks)]
    core = lax.rem(m, 2)
    twin = m + 1 - 2 * core
    same_core = [lax.rem(m + 2 * d, n_blocks) for d in range(1, n_blocks // 2)]
    cousins = [(lax.rem(g + d, n_groups), who) for d in range(1, n_groups) for who in (m, twin)]
    half = vectors // 2

    barrier = pltpu.get_barrier_semaphore()
    greeted = [left_id, right_id] + peers + cousins
    for who in greeted:
        pl.semaphore_signal(barrier, inc=1, device_id=who, device_id_type=MESH)

    pairs = [
        (skel_block_in, skel_block), (skel_leaf_in, skel_leaf), (skel_group_in, skel_group), (morton_in, morton),
        (points_in, points), (charges_in, charges), (neighbours_in, neighbours), (counts_in, counts),
    ]
    loads = [pltpu.make_async_copy(a, b, in_sem.at[k]) for k, (a, b) in enumerate(pairs)]
    for c in loads:
        c.start()

    def scale(terms):
        return gain_factor / math.sqrt(terms)

    def leaf_cols(i):
        return slice(i * leaf_size, (i + 1) * leaf_size)

    def rank_cols(i):
        return slice(i * rank, (i + 1) * rank)

    def doubled(pad, coords):
        pad[6:8] = jnp.zeros((2, coords.shape[1]), f32)
        pad[0:3] = coords
        pad[3:6] = coords
        return features(pad[...])

    loads[0].wait()
    skel_all[pl.ds(m, 1), 0:3] = skel_block[...][None]
    skel_all[pl.ds(m, 1), 3:4] = jnp.zeros((1, 1, rank), f32)
    src_b, tgt = doubled(pad_blk.at[0], skel_block[...])
    blk_tgt[...] = tgt.astype(bf16)
    loads[1].wait()
    src, tgt = doubled(pad_leaf, skel_leaf[...])
    leaf_src[...] = src.T.astype(bf16)
    leaf_tgt[...] = tgt.astype(bf16)
    fill_kernel(leaf_src[...], blk_tgt[...], kl_hi, kl_lo, 0, 0)
    loads[2].wait()
    src, tgt = doubled(pad_grp, skel_group[...])
    grp_src[...] = src.T.astype(bf16)
    for j in range(n_groups):
        pl.when(g == j)(functools.partial(
            grp_tgt.__setitem__, (slice(None), slice(None)), tgt[:, rank_cols(j)].astype(bf16)))
    fill_kernel(src_b.T.astype(bf16), grp_tgt[...], kr_hi, kr_lo, 0, 0)

    for c in loads[3:6]:
        c.wait()
    pad_pts[6:8] = jnp.zeros((2, block_pts), f32)
    pad_pts[0:3] = points[...]
    pad_pts[3:6] = points[...]
    pts = pad_pts[...]
    stacked = jnp.concatenate(
        parts(pts, 3) + [jnp.zeros_like(pts)] + parts(charges[...], 2), axis=0
    ).astype(bf16)
    place = lax.broadcasted_iota(jnp.int32, (leaf_size, leaf_size), 0)
    for i in range(leaf_count):
        s = jnp.zeros((stacked.shape[0], leaf_size), f32)
        for r in range(0, block_pts, leaf_size):
            onehot = jnp.where(place == morton[0:1, leaf_cols(i)] - r, 1.0, 0.0).astype(bf16)
            s = s + jnp.dot(stacked[:, r : r + leaf_size], onehot, preferred_element_type=f32)
        sorted_pts[:, leaf_cols(i)] = s[0:8] + s[8:16] + s[16:24]
        chg_out[:, leaf_cols(i)] = s[32 : 32 + vectors] + s[32 + vectors :]
    pts_out[...] = sorted_pts[0:SENT]

    def to_peer(src, dst, send, recv, who):
        return pltpu.make_async_remote_copy(
            src_ref=src, dst_ref=dst, send_sem=send, recv_sem=recv, device_id=who, device_id_type=MESH)

    def skel_copy(k, who, slot):
        return to_peer(skel_all.at[slot], skel_all.at[slot], skel_send.at[k], skel_recv.at[slot], who)

    to_right = [
        to_peer(pts_out, pts_left, halo_send.at[0], halo_recv.at[0], right_id),
        to_peer(chg_out, chg_left, halo_send.at[1], halo_recv.at[1], right_id),
    ]
    to_left = [
        to_peer(pts_out, pts_right, halo_send.at[2], halo_recv.at[2], left_id),
        to_peer(chg_out, chg_right, halo_send.at[3], halo_recv.at[3], left_id),
    ]
    has_left, has_right = block > 0, block < total - 1

    pl.semaphore_wait(barrier, len(greeted))
    skel_copies = [skel_copy(k, who, m) for k, who in enumerate(peers)]
    for c in skel_copies:
        c.start()

    @pl.when(has_right)
    def _():
        for c in to_right:
            c.start()

    @pl.when(has_left)
    def _():
        for c in to_left:
            c.start()

    src, tgt = features(sorted_pts[...])
    ext_src[block_pts : 2 * block_pts] = src.T.astype(bf16)
    own_tgt[...] = tgt.astype(bf16)
    leaf_w = []
    for i in range(leaf_count):
        fill_kernel(ext_src[leaf_cols(leaf_count + i)], leaf_tgt[:, rank_cols(i)], kp_hi, kp_lo, i * leaf_size, 0)
        leaf_w.append(times_kernel(split_rows(chg_out[:, leaf_cols(i)]), kp_hi[leaf_cols(i)], kp_lo[leaf_cols(i)]))
    lw = jnp.concatenate(leaf_w, axis=1) * scale(leaf_size)
    bw = times_kernel(split_rows(lw), kl_hi[...], kl_lo[...]) * scale(leaf_count * rank)
    bw_all[pl.ds(m, 1)] = bw[None]
    up = times_kernel(split_rows(bw), kr_hi[...], kr_lo[...]) * scale(n_blocks * rank)
    up_out[0] = up[:half]
    up_out[1] = up[half:]

    def up_copy(k, who, slot):
        return to_peer(up_out.at[lax.rem(who[1], 2)], up_in.at[slot], up_send.at[k], up_recv.at[slot], who)

    def bw_copy(k, who, slot):
        return to_peer(bw_all.at[slot], bw_all.at[slot], bw_send.at[k], bw_recv.at[slot], (g, who))

    def gw_copy(k, who, group, part):
        return to_peer(gw_out, gw_all.at[group, part], gw_send.at[k], gw_recv.at[group, part], who)

    up_copies = [up_copy(k, who, m) for k, who in enumerate(peers)]
    bw_copies = [bw_copy(k, who, m) for k, who in enumerate([twin] + same_core)]
    for c in up_copies + bw_copies:
        c.start()

    ext_c[:, block_pts : 2 * block_pts] = chg_out[...]
    loads[6].wait()
    loads[7].wait()
    first_leaf = block * leaf_count - leaf_count

    def values(i, e):
        piece = ext_c[:, leaf_cols(e)]
        if e == leaf_count + i:
            return piece
        times = jnp.int32(0)
        for k in range(slots):
            hit = (neighbours[i, k] - first_leaf == e) & (k < counts[i])
            times = times + jnp.where(hit, 1, 0)
        return piece * times.astype(f32)

    def joined(pieces):
        return split_rows(jnp.concatenate(pieces, axis=1))

    near = []
    for i in range(leaf_count):
        rows = (i + 1) * leaf_size
        fill_kernel(
            ext_src[block_pts : block_pts + rows], own_tgt[:, leaf_cols(i)], kn_hi.at[i], kn_lo.at[i], 0, 0)
    for i in range(leaf_count):
        rows = (i + 1) * leaf_size
        v2 = joined([values(i, leaf_count + j) for j in range(i + 1)])
        acc = times_kernel(v2, kn_hi[i, 0:rows], kn_lo[i, 0:rows])
        for j in range(i + 1, leaf_count):
            acc = acc + times_kernel(
                split_rows(values(i, leaf_count + j)), kn_hi[j, leaf_cols(i)], kn_lo[j, leaf_cols(i)], 1)
        near.append(acc)

    gw = up_out[pl.ds(core, 1)][0]
    for j, c in enumerate(peers):
        up_copy(j, c, c[1]).wait_recv()
        gw = gw + up_in[pl.ds(c[1], 1)][0]
    gw_out[...] = gw
    gw_copies = [gw_copy(k, who, g, core) for k, who in enumerate(cousins)]
    for c in gw_copies:
        c.start()
    forwards = []
    for k, c in enumerate(same_core):
        bw_copy(0, twin, c).wait_recv()
        forwards.append(bw_copy(1 + len(same_core) + k, twin, c))
        forwards[-1].start()

    empty = jnp.zeros((vectors, rank), f32)

    def cousin_rows(d):
        return pl.ds(pl.multiple_of(lax.rem(g + d, n_groups) * rank, rank), rank)

    def fill_group(d):
        fill_kernel(grp_src[cousin_rows(d)], grp_tgt[...], kg_hi.at[d - 1], kg_lo.at[d - 1], 0, 0)

    def fill_peer(d):
        src, _ = doubled(pad_blk.at[d], skel_all[lax.rem(m + d, n_blocks)][0:3])
        fill_kernel(src.T.astype(bf16), blk_tgt[...], kb_hi.at[d - 1], kb_lo.at[d - 1], 0, 0)

    def add_peer(d, acc):
        v2 = split_rows(bw_all[lax.rem(m + d, n_blocks)])
        return acc + times_kernel(v2, kb_hi[d - 1], kb_lo[d - 1])

    repeat(n_groups, fill_group)
    for j, c in enumerate(peers):
        skel_copy(j, c, c[1]).wait_recv()
    repeat(n_blocks, fill_peer)

    def halo(there, copies, pts, chg, pad, base):
        @pl.when(there)
        def _():
            for c in copies:
                c.wait_recv()

        @pl.when(jnp.logical_not(there))
        def _():
            pts[...] = jnp.zeros_like(pts)
            chg[...] = jnp.zeros_like(chg)

        src, _ = doubled(pad, pts[0:3])
        ext_src[base : base + block_pts] = src.T.astype(bf16)
        ext_c[:, base : base + block_pts] = chg[...]

    halo(has_left, to_right, pts_left, chg_left, pad_left, 0)
    halo(has_right, to_left, pts_right, chg_right, pad_right, 2 * block_pts)
    for i in range(leaf_count):
        base = leaf_count * leaf_size
        before = list(range(i, leaf_count))
        after = list(range(2 * leaf_count, 2 * leaf_count + i + 1))
        split = base + len(before) * leaf_size
        end = split + len(after) * leaf_size
        target = own_tgt[:, leaf_cols(i)]
        fill_kernel(ext_src[i * leaf_size : block_pts], target, kn_hi.at[i], kn_lo.at[i], base, 0)
        fill_kernel(
            ext_src[2 * block_pts : 2 * block_pts + len(after) * leaf_size], target, kn_hi.at[i], kn_lo.at[i], split, 0)
        v2 = joined([values(i, e) for e in before + after])
        near[i] = near[i] + times_kernel(v2, kn_hi[i, base:end], kn_lo[i, base:end])

    bw_copy(0, twin, twin).wait_recv()
    for c in same_core:
        bw_copy(0, twin, lax.rem(c + twin - m + n_blocks, n_blocks)).wait_recv()
    field = gather_terms(n_blocks, add_peer, empty) * scale((n_blocks - 1) * rank)
    for d in range(1, n_groups):
        for part in range(2):
            gw_copy(0, cousins[0], lax.rem(g + d, n_groups), part).wait_recv()

    def add_group(d, acc):
        h = lax.rem(g + d, n_groups)
        v2 = split_rows(jnp.concatenate([gw_all[h, 0], gw_all[h, 1]], axis=0))
        return acc + times_kernel(v2, kg_hi[d - 1], kg_lo[d - 1])

    gfield = gather_terms(n_groups, add_group, empty) * scale((n_groups - 1) * rank)
    field = field + scale(rank) * times_kernel(split_rows(gfield), kr_hi[...], kr_lo[...], 1)
    lf = times_kernel(split_rows(field), kl_hi[...], kl_lo[...], 1) * scale(rank)
    for i in range(leaf_count):
        far = times_kernel(split_rows(lf[:, rank_cols(i)]), kp_hi[leaf_cols(i)], kp_lo[leaf_cols(i)], 1)
        out[:, leaf_cols(i)] = near[i] * scale(leaf_size) + far * scale(rank)

    @pl.when(has_right)
    def _():
        for c in to_right:
            c.wait_send()

    @pl.when(has_left)
    def _():
        for c in to_left:
            c.wait_send()

    for c in skel_copies + up_copies + bw_copies + forwards + gw_copies:
        c.wait_send()


def body(n_groups, n_blocks, points, charges, morton, neighbours, counts, skel_leaf, skel_block, skel_group):
    vectors, block_pts = charges.shape
    leaf_count = counts.shape[0]
    leaf_size = block_pts // leaf_count
    rank = skel_block.shape[1]
    slots = neighbours.shape[1]
    leaf_cols = leaf_count * rank
    window = (2 * leaf_count + 1) * leaf_size
    dma = pltpu.SemaphoreType.DMA
    morton = morton.reshape(1, block_pts)
    operands = (points, charges, morton, neighbours, counts, skel_leaf, skel_block, skel_group)
    places = (pltpu.VMEM,) * 3 + (pltpu.SMEM,) * 2 + (pltpu.VMEM,) * 3
    both = lambda *shape: [pltpu.VMEM(shape, bf16)] * 2
    return pl.pallas_call(
        functools.partial(kernel, n_groups, n_blocks, leaf_count, leaf_size, rank, slots),
        out_shape=jax.ShapeDtypeStruct((vectors, block_pts), f32),
        in_specs=[pl.BlockSpec(memory_space=pltpu.HBM)] * len(operands),
        out_specs=pl.BlockSpec(memory_space=pltpu.VMEM),
        scratch_shapes=[
            *[place(a.shape, a.dtype) for place, a in zip(places, operands)],
            pltpu.VMEM((ROWS, block_pts), f32),
            pltpu.VMEM((ROWS, leaf_cols), f32),
            pltpu.VMEM((ROWS, n_groups * rank), f32),
            pltpu.VMEM((n_blocks, ROWS, rank), f32),
            pltpu.VMEM((ROWS, block_pts), f32),
            pltpu.VMEM((ROWS, block_pts), f32),
            pltpu.VMEM((ROWS, block_pts), f32),
            pltpu.VMEM((vectors, block_pts), f32),
            pltpu.VMEM((vectors, block_pts), f32),
            pltpu.VMEM((vectors, block_pts), f32),
            pltpu.VMEM((SENT, block_pts), f32),
            pltpu.VMEM((SENT, block_pts), f32),
            pltpu.VMEM((SENT, block_pts), f32),
            pltpu.VMEM((n_blocks, SENT, rank), f32),
            pltpu.VMEM((2, vectors // 2, rank), f32),
            pltpu.VMEM((n_blocks, vectors // 2, rank), f32),
            pltpu.VMEM((n_blocks, vectors, rank), f32),
            pltpu.VMEM((vectors // 2, rank), f32),
            pltpu.VMEM((n_groups, 2, vectors // 2, rank), f32),
            pltpu.VMEM((3 * block_pts, FEAT), bf16),
            pltpu.VMEM((vectors, 3 * block_pts), f32),
            pltpu.VMEM((FEAT, block_pts), bf16),
            pltpu.VMEM((leaf_cols, FEAT), bf16),
            pltpu.VMEM((FEAT, leaf_cols), bf16),
            pltpu.VMEM((n_groups * rank, FEAT), bf16),
            pltpu.VMEM((FEAT, rank), bf16),
            pltpu.VMEM((FEAT, rank), bf16),
            *both(block_pts, rank),
            *both(leaf_cols, rank),
            *both(rank, rank),
            *both(n_blocks - 1, rank, rank),
            *both(n_groups - 1, rank, rank),
            *both(leaf_count, window, leaf_size),
            dma((len(operands),)),
            dma((4,)),
            dma((4,)),
            dma((n_blocks - 1,)),
            dma((n_blocks,)),
            dma((n_blocks - 1,)),
            dma((n_blocks,)),
            dma((n_blocks,)),
            dma((n_blocks,)),
            dma((2 * (n_groups - 1),)),
            dma((n_groups, 2)),
        ],
        compiler_params=pltpu.CompilerParams(
            collective_id=0, has_side_effects=True, vmem_limit_bytes=64 * 1024 * 1024
        ),
    )(*operands)


def solution(mesh):
    return jax.shard_map(
        functools.partial(body, mesh.shape["grp"], mesh.shape["dev"]),
        mesh=mesh,
        in_specs=(
            P(None, ("grp", "dev")),
            P(None, ("grp", "dev")),
            P(("grp", "dev")),
            P(("grp", "dev"), None),
            P(("grp", "dev")),
            P(None, ("grp", "dev")),
            P(None, ("grp", "dev")),
            P(),
        ),
        out_specs=P(None, ("grp", "dev")),
        check_vma=False,
    )
```

```python
import functools
import math

import jax
import jax.numpy as jnp
from jax import lax
from jax.experimental import pallas as pl
from jax.experimental.pallas import tpu as pltpu
from jax.sharding import PartitionSpec as P

width_sq = 0.1
gain_factor = 5.0
to_base_two = math.sqrt(math.log2(math.e) / width_sq)
middle = 1.0
FEAT = 32
ROWS = 8
SENT = 4
MESH = pl.DeviceIdType.MESH
f32, bf16 = jnp.float32, jnp.bfloat16


def parts(x, count):
    out = []
    for _ in range(count - 1):
        out.append(x.astype(bf16).astype(f32))
        x = x - out[-1]
    out.append(x.astype(bf16).astype(f32))
    return out


def features(coords):
    row = lax.broadcasted_iota(jnp.int32, coords.shape, 0)
    low, used = row < 3, row < 6
    c = jnp.where(used, (coords - middle) * to_base_two, 0.0)
    norm = jnp.sum(jnp.where(low, c * c, 0.0), axis=0, keepdims=True)
    norm = jnp.broadcast_to(norm, c.shape)
    hi, mid, lo = parts(c, 3)
    n0, n1, n2 = parts(norm, 3)
    nth = jnp.where((row == 0) | (row == 3), n0, jnp.where((row == 1) | (row == 4), n1, n2))
    src_n = jnp.where(low, nth, jnp.where(used, 1.0, 0.0))
    tgt_n = jnp.where(low, -1.0, jnp.where(used, -nth, 0.0))
    upper = jnp.where(low, hi + hi, mid + mid)
    src = jnp.concatenate([hi, mid, jnp.where(low, hi, lo), src_n], axis=0)
    tgt = jnp.concatenate([upper, upper, jnp.where(low, lo + lo, hi + hi), tgt_n], axis=0)
    return src, tgt


def split_rows(v):
    return jnp.concatenate(parts(v, 2), axis=0).astype(bf16)


CHUNK = 64


def fill_kernel(src, tgt, k_hi, k_lo, row, col):
    for r in range(0, src.shape[0], CHUNK):
        k = jnp.exp2(jnp.dot(src[r : r + CHUNK], tgt, preferred_element_type=f32))
        hi = k.astype(bf16)
        at = (slice(row + r, row + r + CHUNK), slice(col, col + tgt.shape[1]))
        k_hi[at] = hi
        k_lo[at] = (k - hi.astype(f32)).astype(bf16)


def times_kernel(v2, k_hi, k_lo):
    half = v2.shape[0] // 2
    r = jnp.dot(v2, k_hi, preferred_element_type=f32)
    q = jnp.dot(v2[:half], k_lo, preferred_element_type=f32)
    return r[:half] + r[half:] + q


def repeat(number, step):
    if number <= 8:
        for index in range(1, number):
            step(index)
    else:
        lax.fori_loop(1, number, lambda index, carry: (step(index), carry)[1], 0)


def gather_terms(number, step, start):
    if number <= 8:
        for index in range(1, number):
            start = step(index, start)
        return start
    return lax.fori_loop(1, number, step, start)


def kernel(
    n_groups, n_blocks, leaf_count, leaf_size, rank, slots,
    points_in, charges_in, morton_in, neighbours_in, counts_in, skel_leaf_in, skel_block_in, skel_group_in,
    out,
    points, charges, morton, neighbours, counts, skel_leaf, skel_block, skel_group,
    pad_pts, pad_leaf, pad_grp, pad_blk, pad_left, pad_right, sorted_pts, chg_out, chg_left, chg_right,
    pts_out, pts_left, pts_right, up_out, up_in, bw_all, gw_out, gw_all,
    ext_src, ext_c, own_tgt, leaf_src, leaf_tgt, grp_src, grp_tgt, blk_tgt,
    kp_hi, kp_lo, kl_hi, kl_lo, kr_hi, kr_lo, kb_hi, kb_lo, kg_hi, kg_lo, kn_hi, kn_lo,
    kd_hi, kd_lo, kc_hi, kc_lo, kt_hi, kt_lo,
    in_sem, halo_send, halo_recv, up_send, up_recv, bw_send, bw_recv, gw_send, gw_recv,
):
    vectors, block_pts = charges.shape
    g = lax.axis_index("grp")
    m = lax.axis_index("dev")
    block = g * n_blocks + m
    total = n_groups * n_blocks
    right = lax.rem(block + 1, total)
    left = lax.rem(block + total - 1, total)
    right_id = (right // n_blocks, lax.rem(right, n_blocks))
    left_id = (left // n_blocks, lax.rem(left, n_blocks))
    peers = [(g, lax.rem(m + d, n_blocks)) for d in range(1, n_blocks)]
    core = lax.rem(m, 2)
    twin = m + 1 - 2 * core
    same_core = [lax.rem(m + 2 * d, n_blocks) for d in range(1, n_blocks // 2)]
    cousins = [(lax.rem(g + d, n_groups), who) for d in range(1, n_groups) for who in (m, twin)]
    half = vectors // 2

    barrier = pltpu.get_barrier_semaphore()
    greeted = [left_id, right_id] + peers + cousins
    for who in greeted:
        pl.semaphore_signal(barrier, inc=1, device_id=who, device_id_type=MESH)

    pairs = [
        (skel_block_in, skel_block), (skel_leaf_in, skel_leaf), (skel_group_in, skel_group), (morton_in, morton),
        (points_in, points), (charges_in, charges), (neighbours_in, neighbours), (counts_in, counts),
    ]
    loads = [pltpu.make_async_copy(a, b, in_sem.at[k]) for k, (a, b) in enumerate(pairs)]
    for c in loads:
        c.start()

    def scale(terms):
        return gain_factor / math.sqrt(terms)

    def leaf_cols(i):
        return slice(i * leaf_size, (i + 1) * leaf_size)

    def rank_cols(i):
        return slice(i * rank, (i + 1) * rank)

    def doubled(pad, coords):
        pad[6:8] = jnp.zeros((2, coords.shape[1]), f32)
        pad[0:3] = coords
        pad[3:6] = coords
        return features(pad[...])

    loads[0].wait()
    src_b, tgt = doubled(pad_blk, skel_block[...])
    bw_all[pl.ds(m, 1), vectors:] = pad_blk[...][None]
    blk_tgt[...] = tgt.astype(bf16)
    loads[1].wait()
    src, tgt = doubled(pad_leaf, skel_leaf[...])
    leaf_src[...] = src.T.astype(bf16)
    leaf_tgt[...] = tgt.astype(bf16)
    fill_kernel(leaf_src[...], blk_tgt[...], kl_hi, kl_lo, 0, 0)
    loads[2].wait()
    src, tgt = doubled(pad_grp, skel_group[...])
    grp_src[...] = src.T.astype(bf16)
    for j in range(n_groups):
        pl.when(g == j)(functools.partial(
            grp_tgt.__setitem__, (slice(None), slice(None)), tgt[:, rank_cols(j)].astype(bf16)))
    fill_kernel(src_b.T.astype(bf16), grp_tgt[...], kr_hi, kr_lo, 0, 0)

    for c in loads[3:6]:
        c.wait()
    pad_pts[6:8] = jnp.zeros((2, block_pts), f32)
    pad_pts[0:3] = points[...]
    pad_pts[3:6] = points[...]
    pts = pad_pts[...]
    stacked = jnp.concatenate(
        parts(pts, 3) + [jnp.zeros_like(pts)] + parts(charges[...], 2), axis=0
    ).astype(bf16)
    place = lax.broadcasted_iota(jnp.int32, (leaf_size, leaf_size), 0)
    for i in range(leaf_count):
        s = jnp.zeros((stacked.shape[0], leaf_size), f32)
        for r in range(0, block_pts, leaf_size):
            onehot = jnp.where(place == morton[0:1, leaf_cols(i)] - r, 1.0, 0.0).astype(bf16)
            s = s + jnp.dot(stacked[:, r : r + leaf_size], onehot, preferred_element_type=f32)
        sorted_pts[:, leaf_cols(i)] = s[0:8] + s[8:16] + s[16:24]
        chg_out[:, leaf_cols(i)] = s[32 : 32 + vectors] + s[32 + vectors :]
    pts_out[...] = sorted_pts[0:SENT]

    def to_peer(src, dst, send, recv, who):
        return pltpu.make_async_remote_copy(
            src_ref=src, dst_ref=dst, send_sem=send, recv_sem=recv, device_id=who, device_id_type=MESH)

    to_right = [
        to_peer(pts_out, pts_left, halo_send.at[0], halo_recv.at[0], right_id),
        to_peer(chg_out, chg_left, halo_send.at[1], halo_recv.at[1], right_id),
    ]
    to_left = [
        to_peer(pts_out, pts_right, halo_send.at[2], halo_recv.at[2], left_id),
        to_peer(chg_out, chg_right, halo_send.at[3], halo_recv.at[3], left_id),
    ]
    has_left, has_right = block > 0, block < total - 1

    pl.semaphore_wait(barrier, len(greeted))

    @pl.when(has_right)
    def _():
        for c in to_right:
            c.start()

    @pl.when(has_left)
    def _():
        for c in to_left:
            c.start()

    src, tgt = features(sorted_pts[...])
    ext_src[block_pts : 2 * block_pts] = src.T.astype(bf16)
    own_tgt[...] = tgt.astype(bf16)
    leaf_w = []
    for i in range(leaf_count):
        fill_kernel(ext_src[leaf_cols(leaf_count + i)], leaf_tgt[:, rank_cols(i)], kp_hi, kp_lo, i * leaf_size, 0)
        leaf_w.append(times_kernel(split_rows(chg_out[:, leaf_cols(i)]), kp_hi[leaf_cols(i)], kp_lo[leaf_cols(i)]))
    lw = jnp.concatenate(leaf_w, axis=1) * scale(leaf_size)
    bw = times_kernel(split_rows(lw), kl_hi[...], kl_lo[...]) * scale(leaf_count * rank)
    bw_all[pl.ds(m, 1), 0:vectors] = bw[None]
    up = times_kernel(split_rows(bw), kr_hi[...], kr_lo[...]) * scale(n_blocks * rank)
    up_out[0] = up[:half]
    up_out[1] = up[half:]

    def up_copy(k, who, slot):
        return to_peer(up_out.at[lax.rem(who[1], 2)], up_in.at[slot], up_send.at[k], up_recv.at[slot], who)

    def bw_copy(k, who, slot):
        return to_peer(bw_all.at[slot], bw_all.at[slot], bw_send.at[k], bw_recv.at[slot], (g, who))

    def gw_copy(k, who, group, part):
        return to_peer(gw_out, gw_all.at[group, part], gw_send.at[k], gw_recv.at[group, part], who)

    up_copies = [up_copy(k, who, m) for k, who in enumerate(peers)]
    bw_copies = [bw_copy(k, who, m) for k, who in enumerate([twin] + same_core)]
    for c in up_copies + bw_copies:
        c.start()

    ext_c[:, block_pts : 2 * block_pts] = chg_out[...]
    loads[6].wait()
    loads[7].wait()
    first_leaf = block * leaf_count - leaf_count

    def values(i, e):
        piece = ext_c[:, leaf_cols(e)]
        if e == leaf_count + i:
            return piece
        times = jnp.int32(0)
        for k in range(slots):
            hit = (neighbours[i, k] - first_leaf == e) & (k < counts[i])
            times = times + jnp.where(hit, 1, 0)
        return piece * times.astype(f32)

    def joined(pieces):
        return split_rows(jnp.concatenate(pieces, axis=1))

    near = []
    for i in range(leaf_count):
        fill_kernel(
            ext_src[block_pts : 2 * block_pts], own_tgt[:, leaf_cols(i)], kn_hi.at[i], kn_lo.at[i], 0, 0)
        v2 = joined([values(i, leaf_count + j) for j in range(leaf_count)])
        near.append(times_kernel(v2, kn_hi[i, 0:block_pts], kn_lo[i, 0:block_pts]))

    for j, c in enumerate(peers):
        up_copy(j, c, c[1]).wait_recv()
    gw = up_out[pl.ds(core, 1)][0]
    for j, c in enumerate(peers):
        gw = gw + up_in[pl.ds(c[1], 1)][0]
    gw_out[...] = gw
    gw_copies = [gw_copy(k, who, g, core) for k, who in enumerate(cousins)]
    for c in gw_copies:
        c.start()
    forwards = []
    for k, c in enumerate(same_core):
        bw_copy(0, twin, c).wait_recv()
        forwards.append(bw_copy(1 + len(same_core) + k, twin, c))
        forwards[-1].start()

    empty = jnp.zeros((vectors, rank), f32)

    def cousin_rows(d):
        return pl.ds(pl.multiple_of(lax.rem(g + d, n_groups) * rank, rank), rank)

    def fill_group(d):
        fill_kernel(grp_src[cousin_rows(d)], grp_tgt[...], kg_hi.at[d - 1], kg_lo.at[d - 1], 0, 0)

    def fill_peer(d):
        src, _ = features(bw_all[lax.rem(m + d, n_blocks)][vectors:])
        fill_kernel(src.T.astype(bf16), blk_tgt[...], kb_hi.at[d - 1], kb_lo.at[d - 1], 0, 0)

    def add_peer(d, acc):
        v2 = split_rows(bw_all[lax.rem(m + d, n_blocks)][:vectors])
        return acc + times_kernel(v2, kb_hi[d - 1], kb_lo[d - 1])

    repeat(n_groups, fill_group)
    blk_src = src_b.T.astype(bf16)
    own_rows = pl.ds(pl.multiple_of(g * rank, rank), rank)
    fill_kernel(grp_src[own_rows], blk_tgt[...], kd_hi, kd_lo, 0, 0)
    for i in range(leaf_count):
        fill_kernel(blk_src, leaf_tgt[:, rank_cols(i)], kc_hi, kc_lo, 0, i * rank)
        fill_kernel(leaf_src[rank_cols(i)], own_tgt[:, leaf_cols(i)], kt_hi, kt_lo, i * rank, 0)

    def halo(there, copies, pts, chg, pad, base):
        @pl.when(there)
        def _():
            for c in copies:
                c.wait_recv()

        @pl.when(jnp.logical_not(there))
        def _():
            pts[...] = jnp.zeros_like(pts)
            chg[...] = jnp.zeros_like(chg)

        src, _ = doubled(pad, pts[0:3])
        ext_src[base : base + block_pts] = src.T.astype(bf16)
        ext_c[:, base : base + block_pts] = chg[...]

    halo(has_left, to_right, pts_left, chg_left, pad_left, 0)
    halo(has_right, to_left, pts_right, chg_right, pad_right, 2 * block_pts)
    for i in range(leaf_count):
        base = leaf_count * leaf_size
        before = list(range(i, leaf_count))
        after = list(range(2 * leaf_count, 2 * leaf_count + i + 1))
        split = base + len(before) * leaf_size
        end = split + len(after) * leaf_size
        target = own_tgt[:, leaf_cols(i)]
        fill_kernel(ext_src[i * leaf_size : block_pts], target, kn_hi.at[i], kn_lo.at[i], base, 0)
        fill_kernel(
            ext_src[2 * block_pts : 2 * block_pts + len(after) * leaf_size], target, kn_hi.at[i], kn_lo.at[i], split, 0)
        v2 = joined([values(i, e) for e in before + after])
        near[i] = near[i] + times_kernel(v2, kn_hi[i, base:end], kn_lo[i, base:end])

    bw_copy(0, twin, twin).wait_recv()
    for c in same_core:
        bw_copy(0, twin, lax.rem(c + twin - m + n_blocks, n_blocks)).wait_recv()
    repeat(n_blocks, fill_peer)
    field = gather_terms(n_blocks, add_peer, empty) * scale((n_blocks - 1) * rank)
    for d in range(1, n_groups):
        for part in range(2):
            gw_copy(0, cousins[0], lax.rem(g + d, n_groups), part).wait_recv()

    def add_group(d, acc):
        h = lax.rem(g + d, n_groups)
        v2 = split_rows(jnp.concatenate([gw_all[h, 0], gw_all[h, 1]], axis=0))
        return acc + times_kernel(v2, kg_hi[d - 1], kg_lo[d - 1])

    gfield = gather_terms(n_groups, add_group, empty) * scale((n_groups - 1) * rank)
    field = field + scale(rank) * times_kernel(split_rows(gfield), kd_hi[...], kd_lo[...])
    lf = times_kernel(split_rows(field), kc_hi[...], kc_lo[...]) * scale(rank)
    for i in range(leaf_count):
        far = times_kernel(split_rows(lf[:, rank_cols(i)]), kt_hi[rank_cols(i)], kt_lo[rank_cols(i)])
        out[:, leaf_cols(i)] = near[i] * scale(leaf_size) + far * scale(rank)

    @pl.when(has_right)
    def _():
        for c in to_right:
            c.wait_send()

    @pl.when(has_left)
    def _():
        for c in to_left:
            c.wait_send()

    for c in up_copies + bw_copies + forwards + gw_copies:
        c.wait_send()


def body(n_groups, n_blocks, points, charges, morton, neighbours, counts, skel_leaf, skel_block, skel_group):
    vectors, block_pts = charges.shape
    leaf_count = counts.shape[0]
    leaf_size = block_pts // leaf_count
    rank = skel_block.shape[1]
    slots = neighbours.shape[1]
    leaf_cols = leaf_count * rank
    window = (2 * leaf_count + 1) * leaf_size
    dma = pltpu.SemaphoreType.DMA
    morton = morton.reshape(1, block_pts)
    operands = (points, charges, morton, neighbours, counts, skel_leaf, skel_block, skel_group)
    places = (pltpu.VMEM,) * 3 + (pltpu.SMEM,) * 2 + (pltpu.VMEM,) * 3
    both = lambda *shape: [pltpu.VMEM(shape, bf16)] * 2
    return pl.pallas_call(
        functools.partial(kernel, n_groups, n_blocks, leaf_count, leaf_size, rank, slots),
        out_shape=jax.ShapeDtypeStruct((vectors, block_pts), f32),
        in_specs=[pl.BlockSpec(memory_space=pltpu.HBM)] * len(operands),
        out_specs=pl.BlockSpec(memory_space=pltpu.VMEM),
        scratch_shapes=[
            *[place(a.shape, a.dtype) for place, a in zip(places, operands)],
            pltpu.VMEM((ROWS, block_pts), f32),
            pltpu.VMEM((ROWS, leaf_cols), f32),
            pltpu.VMEM((ROWS, n_groups * rank), f32),
            pltpu.VMEM((ROWS, rank), f32),
            pltpu.VMEM((ROWS, block_pts), f32),
            pltpu.VMEM((ROWS, block_pts), f32),
            pltpu.VMEM((ROWS, block_pts), f32),
            pltpu.VMEM((vectors, block_pts), f32),
            pltpu.VMEM((vectors, block_pts), f32),
            pltpu.VMEM((vectors, block_pts), f32),
            pltpu.VMEM((SENT, block_pts), f32),
            pltpu.VMEM((SENT, block_pts), f32),
            pltpu.VMEM((SENT, block_pts), f32),
            pltpu.VMEM((2, vectors // 2, rank), f32),
            pltpu.VMEM((n_blocks, vectors // 2, rank), f32),
            pltpu.VMEM((n_blocks, vectors + ROWS, rank), f32),
            pltpu.VMEM((vectors // 2, rank), f32),
            pltpu.VMEM((n_groups, 2, vectors // 2, rank), f32),
            pltpu.VMEM((3 * block_pts, FEAT), bf16),
            pltpu.VMEM((vectors, 3 * block_pts), f32),
            pltpu.VMEM((FEAT, block_pts), bf16),
            pltpu.VMEM((leaf_cols, FEAT), bf16),
            pltpu.VMEM((FEAT, leaf_cols), bf16),
            pltpu.VMEM((n_groups * rank, FEAT), bf16),
            pltpu.VMEM((FEAT, rank), bf16),
            pltpu.VMEM((FEAT, rank), bf16),
            *both(block_pts, rank),
            *both(leaf_cols, rank),
            *both(rank, rank),
            *both(n_blocks - 1, rank, rank),
            *both(n_groups - 1, rank, rank),
            *both(leaf_count, window, leaf_size),
            *both(rank, rank),
            *both(rank, leaf_cols),
            *both(leaf_cols, leaf_size),
            dma((len(operands),)),
            dma((4,)),
            dma((4,)),
            dma((n_blocks - 1,)),
            dma((n_blocks,)),
            dma((n_blocks,)),
            dma((n_blocks,)),
            dma((2 * (n_groups - 1),)),
            dma((n_groups, 2)),
        ],
        compiler_params=pltpu.CompilerParams(
            collective_id=0, has_side_effects=True, vmem_limit_bytes=64 * 1024 * 1024
        ),
    )(*operands)


def solution(mesh):
    return jax.shard_map(
        functools.partial(body, mesh.shape["grp"], mesh.shape["dev"]),
        mesh=mesh,
        in_specs=(
            P(None, ("grp", "dev")),
            P(None, ("grp", "dev")),
            P(("grp", "dev")),
            P(("grp", "dev"), None),
            P(("grp", "dev")),
            P(None, ("grp", "dev")),
            P(None, ("grp", "dev")),
            P(),
        ),
        out_specs=P(None, ("grp", "dev")),
        check_vma=False,
    )
```

```python
import functools
import math

import jax
import jax.numpy as jnp
from jax import lax
from jax.experimental import pallas as pl
from jax.experimental.pallas import tpu as pltpu
from jax.sharding import PartitionSpec as P

width_sq = 0.1
gain_factor = 5.0
to_base_two = math.sqrt(math.log2(math.e) / width_sq)
middle = 1.0
FEAT = 32
ROWS = 8
SENT = 4
MESH = pl.DeviceIdType.MESH
f32, bf16 = jnp.float32, jnp.bfloat16


def parts(x, count):
    out = []
    for _ in range(count - 1):
        out.append(x.astype(bf16).astype(f32))
        x = x - out[-1]
    out.append(x.astype(bf16).astype(f32))
    return out


def features(coords):
    row = lax.broadcasted_iota(jnp.int32, coords.shape, 0)
    low, used = row < 3, row < 6
    c = jnp.where(used, (coords - middle) * to_base_two, 0.0)
    norm = jnp.sum(jnp.where(low, c * c, 0.0), axis=0, keepdims=True)
    norm = jnp.broadcast_to(norm, c.shape)
    hi, mid, lo = parts(c, 3)
    n0, n1, n2 = parts(norm, 3)
    nth = jnp.where((row == 0) | (row == 3), n0, jnp.where((row == 1) | (row == 4), n1, n2))
    src_n = jnp.where(low, nth, jnp.where(used, 1.0, 0.0))
    tgt_n = jnp.where(low, -1.0, jnp.where(used, -nth, 0.0))
    upper = jnp.where(low, hi + hi, mid + mid)
    src = jnp.concatenate([hi, mid, jnp.where(low, hi, lo), src_n], axis=0)
    tgt = jnp.concatenate([upper, upper, jnp.where(low, lo + lo, hi + hi), tgt_n], axis=0)
    return src, tgt


def split_rows(v):
    return jnp.concatenate(parts(v, 2), axis=0).astype(bf16)


CHUNK = 64


def fill_kernel(src, tgt, k_hi, k_lo, row, col):
    for r in range(0, src.shape[0], CHUNK):
        k = jnp.exp2(jnp.dot(src[r : r + CHUNK], tgt, preferred_element_type=f32))
        hi = k.astype(bf16)
        at = (slice(row + r, row + r + CHUNK), slice(col, col + tgt.shape[1]))
        k_hi[at] = hi
        k_lo[at] = (k - hi.astype(f32)).astype(bf16)


def times_kernel(v2, k_hi, k_lo):
    half = v2.shape[0] // 2
    r = jnp.dot(v2, k_hi, preferred_element_type=f32)
    q = jnp.dot(v2[:half], k_lo, preferred_element_type=f32)
    return r[:half] + r[half:] + q


def repeat(number, step):
    if number <= 8:
        for index in range(1, number):
            step(index)
    else:
        lax.fori_loop(1, number, lambda index, carry: (step(index), carry)[1], 0)


def gather_terms(number, step, start):
    if number <= 8:
        for index in range(1, number):
            start = step(index, start)
        return start
    return lax.fori_loop(1, number, step, start)


def kernel(
    n_groups, n_blocks, leaf_count, leaf_size, rank, slots,
    points_in, charges_in, morton_in, neighbours_in, counts_in, skel_leaf_in, skel_block_in, skel_group_in,
    out,
    points, charges, morton, neighbours, counts, skel_leaf, skel_block, skel_group,
    pad_pts, pad_leaf, pad_grp, pad_own, pad_blk, pad_left, pad_right, sorted_pts, chg_out, chg_left, chg_right,
    pts_out, pts_left, pts_right, up_out, up_in, bw_all, gw_out, gw_all,
    ext_src, ext_c, own_tgt, leaf_src, leaf_tgt, grp_src, grp_tgt, blk_tgt,
    kp_hi, kp_lo, kl_hi, kl_lo, kr_hi, kr_lo, kb_hi, kb_lo, kg_hi, kg_lo, kn_hi, kn_lo,
    kd_hi, kd_lo, kc_hi, kc_lo, kt_hi, kt_lo,
    in_sem, halo_send, halo_recv, up_send, up_recv, bw_send, bw_recv, gw_send, gw_recv,
):
    vectors, block_pts = charges.shape
    g = lax.axis_index("grp")
    m = lax.axis_index("dev")
    block = g * n_blocks + m
    total = n_groups * n_blocks
    right = lax.rem(block + 1, total)
    left = lax.rem(block + total - 1, total)
    right_id = (right // n_blocks, lax.rem(right, n_blocks))
    left_id = (left // n_blocks, lax.rem(left, n_blocks))
    peers = [(g, lax.rem(m + d, n_blocks)) for d in range(1, n_blocks)]
    core = lax.rem(m, 2)
    twin = m + 1 - 2 * core
    same_core = [lax.rem(m + 2 * d, n_blocks) for d in range(1, n_blocks // 2)]
    cousins = [(lax.rem(g + d, n_groups), who) for d in range(1, n_groups) for who in (m, twin)]
    half = vectors // 2

    barrier = pltpu.get_barrier_semaphore()
    greeted = [left_id, right_id] + peers + cousins
    for who in greeted:
        pl.semaphore_signal(barrier, inc=1, device_id=who, device_id_type=MESH)

    pairs = [
        (skel_block_in, skel_block), (skel_leaf_in, skel_leaf), (skel_group_in, skel_group), (morton_in, morton),
        (points_in, points), (charges_in, charges), (neighbours_in, neighbours), (counts_in, counts),
    ]
    loads = [pltpu.make_async_copy(a, b, in_sem.at[k]) for k, (a, b) in enumerate(pairs)]
    for c in loads:
        c.start()

    def scale(terms):
        return gain_factor / math.sqrt(terms)

    def leaf_cols(i):
        return slice(i * leaf_size, (i + 1) * leaf_size)

    def rank_cols(i):
        return slice(i * rank, (i + 1) * rank)

    def doubled(pad, coords):
        pad[6:8] = jnp.zeros((2, coords.shape[1]), f32)
        pad[0:3] = coords
        pad[3:6] = coords
        return features(pad[...])

    for c in loads:
        c.wait()
    pad_pts[6:8] = jnp.zeros((2, block_pts), f32)
    pad_pts[0:3] = points[...]
    pad_pts[3:6] = points[...]
    pts = pad_pts[...]
    stacked = jnp.concatenate(
        parts(pts, 3) + [jnp.zeros_like(pts)] + parts(charges[...], 2), axis=0
    ).astype(bf16)
    place = lax.broadcasted_iota(jnp.int32, (leaf_size, leaf_size), 0)
    for i in range(leaf_count):
        s = jnp.zeros((stacked.shape[0], leaf_size), f32)
        for r in range(0, block_pts, leaf_size):
            onehot = jnp.where(place == morton[0:1, leaf_cols(i)] - r, 1.0, 0.0).astype(bf16)
            s = s + jnp.dot(stacked[:, r : r + leaf_size], onehot, preferred_element_type=f32)
        sorted_pts[:, leaf_cols(i)] = s[0:8] + s[8:16] + s[16:24]
        chg_out[:, leaf_cols(i)] = s[32 : 32 + vectors] + s[32 + vectors :]
    pts_out[...] = sorted_pts[0:SENT]

    own_rows = pl.ds(pl.multiple_of(g * rank, rank), rank)
    src_b, tgt = doubled(pad_blk, skel_block[...])
    bw_all[pl.ds(m, 1), vectors:] = pad_blk[...][None]
    blk_tgt[...] = tgt.astype(bf16)
    blk_src = src_b.T.astype(bf16)
    src, tgt = doubled(pad_leaf, skel_leaf[...])
    leaf_src[...] = src.T.astype(bf16)
    leaf_tgt[...] = tgt.astype(bf16)
    _, tgt = doubled(pad_own, skel_group[:, own_rows])
    grp_tgt[...] = tgt.astype(bf16)
    fill_kernel(leaf_src[...], blk_tgt[...], kl_hi, kl_lo, 0, 0)
    fill_kernel(blk_src, grp_tgt[...], kr_hi, kr_lo, 0, 0)

    src, tgt = features(sorted_pts[...])
    ext_src[block_pts : 2 * block_pts] = src.T.astype(bf16)
    own_tgt[...] = tgt.astype(bf16)
    leaf_w = []
    for i in range(leaf_count):
        fill_kernel(ext_src[leaf_cols(leaf_count + i)], leaf_tgt[:, rank_cols(i)], kp_hi, kp_lo, i * leaf_size, 0)
        leaf_w.append(times_kernel(split_rows(chg_out[:, leaf_cols(i)]), kp_hi[leaf_cols(i)], kp_lo[leaf_cols(i)]))
    lw = jnp.concatenate(leaf_w, axis=1) * scale(leaf_size)
    bw = times_kernel(split_rows(lw), kl_hi[...], kl_lo[...]) * scale(leaf_count * rank)
    bw_all[pl.ds(m, 1), 0:vectors] = bw[None]
    up = times_kernel(split_rows(bw), kr_hi[...], kr_lo[...]) * scale(n_blocks * rank)
    up_out[0] = up[:half]
    up_out[1] = up[half:]

    def to_peer(src, dst, send, recv, who):
        return pltpu.make_async_remote_copy(
            src_ref=src, dst_ref=dst, send_sem=send, recv_sem=recv, device_id=who, device_id_type=MESH)

    to_right = [
        to_peer(pts_out, pts_left, halo_send.at[0], halo_recv.at[0], right_id),
        to_peer(chg_out, chg_left, halo_send.at[1], halo_recv.at[1], right_id),
    ]
    to_left = [
        to_peer(pts_out, pts_right, halo_send.at[2], halo_recv.at[2], left_id),
        to_peer(chg_out, chg_right, halo_send.at[3], halo_recv.at[3], left_id),
    ]
    has_left, has_right = block > 0, block < total - 1

    def up_copy(k, who, slot):
        return to_peer(up_out.at[lax.rem(who[1], 2)], up_in.at[slot], up_send.at[k], up_recv.at[slot], who)

    def bw_copy(k, who, slot):
        return to_peer(bw_all.at[slot], bw_all.at[slot], bw_send.at[k], bw_recv.at[slot], (g, who))

    def gw_copy(k, who, group, part):
        return to_peer(gw_out, gw_all.at[group, part], gw_send.at[k], gw_recv.at[group, part], who)

    up_copies = [up_copy(k, who, m) for k, who in enumerate(peers)]
    bw_copies = [bw_copy(k, who, m) for k, who in enumerate([twin] + same_core)]
    pl.semaphore_wait(barrier, len(greeted))
    for c in up_copies + bw_copies:
        c.start()

    @pl.when(has_right)
    def _():
        for c in to_right:
            c.start()

    @pl.when(has_left)
    def _():
        for c in to_left:
            c.start()

    ext_c[:, block_pts : 2 * block_pts] = chg_out[...]
    first_leaf = block * leaf_count - leaf_count

    def values(i, e):
        piece = ext_c[:, leaf_cols(e)]
        if e == leaf_count + i:
            return piece
        times = jnp.int32(0)
        for k in range(slots):
            hit = (neighbours[i, k] - first_leaf == e) & (k < counts[i])
            times = times + jnp.where(hit, 1, 0)
        return piece * times.astype(f32)

    def joined(pieces):
        return split_rows(jnp.concatenate(pieces, axis=1))

    near = []
    for i in range(leaf_count):
        fill_kernel(
            ext_src[block_pts : 2 * block_pts], own_tgt[:, leaf_cols(i)], kn_hi.at[i], kn_lo.at[i], 0, 0)
        v2 = joined([values(i, leaf_count + j) for j in range(leaf_count)])
        near.append(times_kernel(v2, kn_hi[i, 0:block_pts], kn_lo[i, 0:block_pts]))

    src, _ = doubled(pad_grp, skel_group[...])
    grp_src[...] = src.T.astype(bf16)

    def cousin_rows(d):
        return pl.ds(pl.multiple_of(lax.rem(g + d, n_groups) * rank, rank), rank)

    def fill_group(d):
        fill_kernel(grp_src[cousin_rows(d)], grp_tgt[...], kg_hi.at[d - 1], kg_lo.at[d - 1], 0, 0)

    repeat(n_groups, fill_group)
    fill_kernel(grp_src[own_rows], blk_tgt[...], kd_hi, kd_lo, 0, 0)
    for i in range(leaf_count):
        fill_kernel(blk_src, leaf_tgt[:, rank_cols(i)], kc_hi, kc_lo, 0, i * rank)
        fill_kernel(leaf_src[rank_cols(i)], own_tgt[:, leaf_cols(i)], kt_hi, kt_lo, i * rank, 0)

    for j, c in enumerate(peers):
        up_copy(j, c, c[1]).wait_recv()

    gw = up_out[pl.ds(core, 1)][0]
    for j, c in enumerate(peers):
        gw = gw + up_in[pl.ds(c[1], 1)][0]
    gw_out[...] = gw
    gw_copies = [gw_copy(k, who, g, core) for k, who in enumerate(cousins)]
    for c in gw_copies:
        c.start()
    forwards = []
    for k, c in enumerate(same_core):
        bw_copy(0, twin, c).wait_recv()
        forwards.append(bw_copy(1 + len(same_core) + k, twin, c))
        forwards[-1].start()

    empty = jnp.zeros((vectors, rank), f32)

    def fill_peer(d):
        src, _ = features(bw_all[lax.rem(m + d, n_blocks)][vectors:])
        fill_kernel(src.T.astype(bf16), blk_tgt[...], kb_hi.at[d - 1], kb_lo.at[d - 1], 0, 0)

    def add_peer(d, acc):
        v2 = split_rows(bw_all[lax.rem(m + d, n_blocks)][:vectors])
        return acc + times_kernel(v2, kb_hi[d - 1], kb_lo[d - 1])


    def halo(there, copies, pts, chg, pad, base):
        @pl.when(there)
        def _():
            for c in copies:
                c.wait_recv()

        @pl.when(jnp.logical_not(there))
        def _():
            pts[...] = jnp.zeros_like(pts)
            chg[...] = jnp.zeros_like(chg)

        src, _ = doubled(pad, pts[0:3])
        ext_src[base : base + block_pts] = src.T.astype(bf16)
        ext_c[:, base : base + block_pts] = chg[...]

    halo(has_left, to_right, pts_left, chg_left, pad_left, 0)
    halo(has_right, to_left, pts_right, chg_right, pad_right, 2 * block_pts)
    for i in range(leaf_count):
        base = leaf_count * leaf_size
        before = list(range(i, leaf_count))
        after = list(range(2 * leaf_count, 2 * leaf_count + i + 1))
        split = base + len(before) * leaf_size
        end = split + len(after) * leaf_size
        target = own_tgt[:, leaf_cols(i)]
        fill_kernel(ext_src[i * leaf_size : block_pts], target, kn_hi.at[i], kn_lo.at[i], base, 0)
        fill_kernel(
            ext_src[2 * block_pts : 2 * block_pts + len(after) * leaf_size], target, kn_hi.at[i], kn_lo.at[i], split, 0)
        v2 = joined([values(i, e) for e in before + after])
        near[i] = near[i] + times_kernel(v2, kn_hi[i, base:end], kn_lo[i, base:end])

    bw_copy(0, twin, twin).wait_recv()
    for c in same_core:
        bw_copy(0, twin, lax.rem(c + twin - m + n_blocks, n_blocks)).wait_recv()
    repeat(n_blocks, fill_peer)
    field = gather_terms(n_blocks, add_peer, empty) * scale((n_blocks - 1) * rank)
    @pl.when(has_right)
    def _():
        for c in to_right:
            c.wait_send()

    @pl.when(has_left)
    def _():
        for c in to_left:
            c.wait_send()

    for c in up_copies + bw_copies + forwards + gw_copies:
        c.wait_send()

    for d in range(1, n_groups):
        for part in range(2):
            gw_copy(0, cousins[0], lax.rem(g + d, n_groups), part).wait_recv()

    def add_group(d, acc):
        h = lax.rem(g + d, n_groups)
        v2 = split_rows(jnp.concatenate([gw_all[h, 0], gw_all[h, 1]], axis=0))
        return acc + times_kernel(v2, kg_hi[d - 1], kg_lo[d - 1])

    gfield = gather_terms(n_groups, add_group, empty) * scale((n_groups - 1) * rank)
    field = field + scale(rank) * times_kernel(split_rows(gfield), kd_hi[...], kd_lo[...])
    lf = times_kernel(split_rows(field), kc_hi[...], kc_lo[...]) * scale(rank)
    for i in range(leaf_count):
        far = times_kernel(split_rows(lf[:, rank_cols(i)]), kt_hi[rank_cols(i)], kt_lo[rank_cols(i)])
        out[:, leaf_cols(i)] = near[i] * scale(leaf_size) + far * scale(rank)


def body(n_groups, n_blocks, points, charges, morton, neighbours, counts, skel_leaf, skel_block, skel_group):
    vectors, block_pts = charges.shape
    leaf_count = counts.shape[0]
    leaf_size = block_pts // leaf_count
    rank = skel_block.shape[1]
    slots = neighbours.shape[1]
    leaf_cols = leaf_count * rank
    window = (2 * leaf_count + 1) * leaf_size
    dma = pltpu.SemaphoreType.DMA
    morton = morton.reshape(1, block_pts)
    operands = (points, charges, morton, neighbours, counts, skel_leaf, skel_block, skel_group)
    places = (pltpu.VMEM,) * 3 + (pltpu.SMEM,) * 2 + (pltpu.VMEM,) * 3
    both = lambda *shape: [pltpu.VMEM(shape, bf16)] * 2
    return pl.pallas_call(
        functools.partial(kernel, n_groups, n_blocks, leaf_count, leaf_size, rank, slots),
        out_shape=jax.ShapeDtypeStruct((vectors, block_pts), f32),
        in_specs=[pl.BlockSpec(memory_space=pltpu.HBM)] * len(operands),
        out_specs=pl.BlockSpec(memory_space=pltpu.VMEM),
        scratch_shapes=[
            *[place(a.shape, a.dtype) for place, a in zip(places, operands)],
            pltpu.VMEM((ROWS, block_pts), f32),
            pltpu.VMEM((ROWS, leaf_cols), f32),
            pltpu.VMEM((ROWS, n_groups * rank), f32),
            pltpu.VMEM((ROWS, rank), f32),
            pltpu.VMEM((ROWS, rank), f32),
            pltpu.VMEM((ROWS, block_pts), f32),
            pltpu.VMEM((ROWS, block_pts), f32),
            pltpu.VMEM((ROWS, block_pts), f32),
            pltpu.VMEM((vectors, block_pts), f32),
            pltpu.VMEM((vectors, block_pts), f32),
            pltpu.VMEM((vectors, block_pts), f32),
            pltpu.VMEM((SENT, block_pts), f32),
            pltpu.VMEM((SENT, block_pts), f32),
            pltpu.VMEM((SENT, block_pts), f32),
            pltpu.VMEM((2, vectors // 2, rank), f32),
            pltpu.VMEM((n_blocks, vectors // 2, rank), f32),
            pltpu.VMEM((n_blocks, vectors + ROWS, rank), f32),
            pltpu.VMEM((vectors // 2, rank), f32),
            pltpu.VMEM((n_groups, 2, vectors // 2, rank), f32),
            pltpu.VMEM((3 * block_pts, FEAT), bf16),
            pltpu.VMEM((vectors, 3 * block_pts), f32),
            pltpu.VMEM((FEAT, block_pts), bf16),
            pltpu.VMEM((leaf_cols, FEAT), bf16),
            pltpu.VMEM((FEAT, leaf_cols), bf16),
            pltpu.VMEM((n_groups * rank, FEAT), bf16),
            pltpu.VMEM((FEAT, rank), bf16),
            pltpu.VMEM((FEAT, rank), bf16),
            *both(block_pts, rank),
            *both(leaf_cols, rank),
            *both(rank, rank),
            *both(n_blocks - 1, rank, rank),
            *both(n_groups - 1, rank, rank),
            *both(leaf_count, window, leaf_size),
            *both(rank, rank),
            *both(rank, leaf_cols),
            *both(leaf_cols, leaf_size),
            dma((len(operands),)),
            dma((4,)),
            dma((4,)),
            dma((n_blocks - 1,)),
            dma((n_blocks,)),
            dma((n_blocks,)),
            dma((n_blocks,)),
            dma((2 * (n_groups - 1),)),
            dma((n_groups, 2)),
        ],
        compiler_params=pltpu.CompilerParams(
            collective_id=0, has_side_effects=True, vmem_limit_bytes=64 * 1024 * 1024
        ),
    )(*operands)


def solution(mesh):
    return jax.shard_map(
        functools.partial(body, mesh.shape["grp"], mesh.shape["dev"]),
        mesh=mesh,
        in_specs=(
            P(None, ("grp", "dev")),
            P(None, ("grp", "dev")),
            P(("grp", "dev")),
            P(("grp", "dev"), None),
            P(("grp", "dev")),
            P(None, ("grp", "dev")),
            P(None, ("grp", "dev")),
            P(),
        ),
        out_specs=P(None, ("grp", "dev")),
        check_vma=False,
    )
```

```python
import functools
import math

import jax
import jax.numpy as jnp
from jax import lax
from jax.experimental import pallas as pl
from jax.experimental.pallas import tpu as pltpu
from jax.sharding import PartitionSpec as P

width_sq = 0.1
gain_factor = 5.0
to_base_two = math.sqrt(math.log2(math.e) / width_sq)
middle = 1.0
FEAT = 32
ROWS = 8
SENT = 4
MESH = pl.DeviceIdType.MESH
f32, bf16 = jnp.float32, jnp.bfloat16


def parts(x, count):
    out = []
    for _ in range(count - 1):
        out.append(x.astype(bf16).astype(f32))
        x = x - out[-1]
    out.append(x.astype(bf16).astype(f32))
    return out


def features(coords):
    row = lax.broadcasted_iota(jnp.int32, coords.shape, 0)
    low, used = row < 3, row < 6
    c = jnp.where(used, (coords - middle) * to_base_two, 0.0)
    norm = jnp.sum(jnp.where(low, c * c, 0.0), axis=0, keepdims=True)
    norm = jnp.broadcast_to(norm, c.shape)
    hi, mid, lo = parts(c, 3)
    n0, n1, n2 = parts(norm, 3)
    nth = jnp.where((row == 0) | (row == 3), n0, jnp.where((row == 1) | (row == 4), n1, n2))
    src_n = jnp.where(low, nth, jnp.where(used, 1.0, 0.0))
    tgt_n = jnp.where(low, -1.0, jnp.where(used, -nth, 0.0))
    upper = jnp.where(low, hi + hi, mid + mid)
    src = jnp.concatenate([hi, mid, jnp.where(low, hi, lo), src_n], axis=0)
    tgt = jnp.concatenate([upper, upper, jnp.where(low, lo + lo, hi + hi), tgt_n], axis=0)
    return src, tgt


def split_rows(v):
    return jnp.concatenate(parts(v, 2), axis=0).astype(bf16)


CHUNK = 64


def fill_kernel(src, tgt, k_hi, k_lo, row, col):
    for r in range(0, src.shape[0], CHUNK):
        k = jnp.exp2(jnp.dot(src[r : r + CHUNK], tgt, preferred_element_type=f32))
        hi = k.astype(bf16)
        at = (slice(row + r, row + r + CHUNK), slice(col, col + tgt.shape[1]))
        k_hi[at] = hi
        k_lo[at] = (k - hi.astype(f32)).astype(bf16)


def times_kernel(v2, k_hi, k_lo):
    half = v2.shape[0] // 2
    r = jnp.dot(v2, k_hi, preferred_element_type=f32)
    q = jnp.dot(v2[:half], k_lo, preferred_element_type=f32)
    return r[:half] + r[half:] + q


def repeat(number, step):
    if number <= 8:
        for index in range(1, number):
            step(index)
    else:
        lax.fori_loop(1, number, lambda index, carry: (step(index), carry)[1], 0)


def gather_terms(number, step, start):
    if number <= 8:
        for index in range(1, number):
            start = step(index, start)
        return start
    return lax.fori_loop(1, number, step, start)


def kernel(
    n_groups, n_blocks, leaf_count, leaf_size, rank, slots,
    points_in, charges_in, morton_in, neighbours_in, counts_in, skel_leaf_in, skel_block_in, skel_group_in,
    out,
    points, charges, morton, neighbours, counts, skel_leaf, skel_block, skel_group,
    pad_pts, pad_leaf, pad_grp, pad_own, pad_blk, pad_left, pad_right, sorted_pts, chg_out, chg_left, chg_right,
    pts_out, pts_left, pts_right, up_out, up_in, bw_all, gw_out, gw_all,
    ext_src, ext_c, own_tgt, leaf_src, leaf_tgt, grp_src, grp_tgt, blk_tgt,
    kp_hi, kp_lo, kl_hi, kl_lo, kr_hi, kr_lo, kb_hi, kb_lo, kg_hi, kg_lo, kn_hi, kn_lo,
    kd_hi, kd_lo, kc_hi, kc_lo, kt_hi, kt_lo,
    in_sem, halo_send, halo_recv, up_send, up_recv, bw_send, bw_recv, gw_send, gw_recv,
):
    vectors, block_pts = charges.shape
    g = lax.axis_index("grp")
    m = lax.axis_index("dev")
    block = g * n_blocks + m
    total = n_groups * n_blocks
    right = lax.rem(block + 1, total)
    left = lax.rem(block + total - 1, total)
    right_id = (right // n_blocks, lax.rem(right, n_blocks))
    left_id = (left // n_blocks, lax.rem(left, n_blocks))
    peers = [(g, lax.rem(m + d, n_blocks)) for d in range(1, n_blocks)]
    core = lax.rem(m, 2)
    twin = m + 1 - 2 * core
    same_core = [lax.rem(m + 2 * d, n_blocks) for d in range(1, n_blocks // 2)]
    cousins = [(lax.rem(g + d, n_groups), who) for d in range(1, n_groups) for who in (m, twin)]
    half = vectors // 2

    barrier = pltpu.get_barrier_semaphore()
    greeted = [left_id, right_id] + peers + cousins
    for who in greeted:
        pl.semaphore_signal(barrier, inc=1, device_id=who, device_id_type=MESH)

    pairs = [
        (skel_block_in, skel_block), (skel_leaf_in, skel_leaf), (skel_group_in, skel_group), (morton_in, morton),
        (points_in, points), (charges_in, charges), (neighbours_in, neighbours), (counts_in, counts),
    ]
    loads = [pltpu.make_async_copy(a, b, in_sem.at[k]) for k, (a, b) in enumerate(pairs)]
    for c in loads:
        c.start()

    def scale(terms):
        return gain_factor / math.sqrt(terms)

    def leaf_cols(i):
        return slice(i * leaf_size, (i + 1) * leaf_size)

    def rank_cols(i):
        return slice(i * rank, (i + 1) * rank)

    def doubled(pad, coords):
        pad[6:8] = jnp.zeros((2, coords.shape[1]), f32)
        pad[0:3] = coords
        pad[3:6] = coords
        return features(pad[...])

    for c in loads:
        c.wait()
    pad_pts[6:8] = jnp.zeros((2, block_pts), f32)
    pad_pts[0:3] = points[...]
    pad_pts[3:6] = points[...]
    pts = pad_pts[...]
    stacked = jnp.concatenate(
        parts(pts, 3) + [jnp.zeros_like(pts)] + parts(charges[...], 2), axis=0
    ).astype(bf16)
    place = lax.broadcasted_iota(jnp.int32, (leaf_size, leaf_size), 0)
    for i in range(leaf_count):
        s = jnp.zeros((stacked.shape[0], leaf_size), f32)
        for r in range(0, block_pts, leaf_size):
            onehot = jnp.where(place == morton[0:1, leaf_cols(i)] - r, 1.0, 0.0).astype(bf16)
            s = s + jnp.dot(stacked[:, r : r + leaf_size], onehot, preferred_element_type=f32)
        sorted_pts[:, leaf_cols(i)] = s[0:8] + s[8:16] + s[16:24]
        chg_out[:, leaf_cols(i)] = s[32 : 32 + vectors] + s[32 + vectors :]
    pts_out[...] = sorted_pts[0:SENT]

    own_rows = pl.ds(pl.multiple_of(g * rank, rank), rank)
    src_b, tgt = doubled(pad_blk, skel_block[...])
    bw_all[pl.ds(m, 1), vectors:] = pad_blk[...][None]
    blk_tgt[...] = tgt.astype(bf16)
    blk_src = src_b.T.astype(bf16)
    src, tgt = doubled(pad_leaf, skel_leaf[...])
    leaf_src[...] = src.T.astype(bf16)
    leaf_tgt[...] = tgt.astype(bf16)
    _, tgt = doubled(pad_own, skel_group[:, own_rows])
    grp_tgt[...] = tgt.astype(bf16)
    fill_kernel(leaf_src[...], blk_tgt[...], kl_hi, kl_lo, 0, 0)
    fill_kernel(blk_src, grp_tgt[...], kr_hi, kr_lo, 0, 0)

    src, tgt = features(sorted_pts[...])
    ext_src[block_pts : 2 * block_pts] = src.T.astype(bf16)
    own_tgt[...] = tgt.astype(bf16)
    leaf_w = []
    for i in range(leaf_count):
        fill_kernel(ext_src[leaf_cols(leaf_count + i)], leaf_tgt[:, rank_cols(i)], kp_hi, kp_lo, i * leaf_size, 0)
        leaf_w.append(times_kernel(split_rows(chg_out[:, leaf_cols(i)]), kp_hi[leaf_cols(i)], kp_lo[leaf_cols(i)]))
    lw = jnp.concatenate(leaf_w, axis=1) * scale(leaf_size)
    bw = times_kernel(split_rows(lw), kl_hi[...], kl_lo[...]) * scale(leaf_count * rank)
    bw_all[pl.ds(m, 1), 0:vectors] = bw[None]
    up = times_kernel(split_rows(bw), kr_hi[...], kr_lo[...]) * scale(n_blocks * rank)
    up_out[0] = up[:half]
    up_out[1] = up[half:]

    def to_peer(src, dst, send, recv, who):
        return pltpu.make_async_remote_copy(
            src_ref=src, dst_ref=dst, send_sem=send, recv_sem=recv, device_id=who, device_id_type=MESH)

    to_right = [
        to_peer(pts_out, pts_left, halo_send.at[0], halo_recv.at[0], right_id),
        to_peer(chg_out, chg_left, halo_send.at[1], halo_recv.at[1], right_id),
    ]
    to_left = [
        to_peer(pts_out, pts_right, halo_send.at[2], halo_recv.at[2], left_id),
        to_peer(chg_out, chg_right, halo_send.at[3], halo_recv.at[3], left_id),
    ]
    has_left, has_right = block > 0, block < total - 1

    def up_copy(k, who, slot):
        return to_peer(up_out.at[lax.rem(who[1], 2)], up_in.at[slot], up_send.at[k], up_recv.at[slot], who)

    def bw_copy(k, who, slot):
        return to_peer(bw_all.at[slot], bw_all.at[slot], bw_send.at[k], bw_recv.at[slot], (g, who))

    def gw_copy(k, who, group, part):
        return to_peer(gw_out, gw_all.at[group, part], gw_send.at[k], gw_recv.at[group, part], who)

    up_copies = [up_copy(k, who, m) for k, who in enumerate(peers)]
    bw_copies = [bw_copy(k, who, m) for k, who in enumerate([twin] + same_core)]
    pl.semaphore_wait(barrier, len(greeted))
    for c in up_copies:
        c.start()

    @pl.when(has_right)
    def _():
        for c in to_right:
            c.start()

    @pl.when(has_left)
    def _():
        for c in to_left:
            c.start()

    for c in bw_copies:
        c.start()

    ext_c[:, block_pts : 2 * block_pts] = chg_out[...]
    first_leaf = block * leaf_count - leaf_count

    def values(i, e):
        piece = ext_c[:, leaf_cols(e)]
        if e == leaf_count + i:
            return piece
        times = jnp.int32(0)
        for k in range(slots):
            hit = (neighbours[i, k] - first_leaf == e) & (k < counts[i])
            times = times + jnp.where(hit, 1, 0)
        return piece * times.astype(f32)

    def joined(pieces):
        return split_rows(jnp.concatenate(pieces, axis=1))

    near = []
    for i in range(leaf_count):
        fill_kernel(
            ext_src[block_pts : 2 * block_pts], own_tgt[:, leaf_cols(i)], kn_hi.at[i], kn_lo.at[i], 0, 0)
        v2 = joined([values(i, leaf_count + j) for j in range(leaf_count)])
        near.append(times_kernel(v2, kn_hi[i, 0:block_pts], kn_lo[i, 0:block_pts]))

    src, _ = doubled(pad_grp, skel_group[...])
    grp_src[...] = src.T.astype(bf16)

    def cousin_rows(d):
        return pl.ds(pl.multiple_of(lax.rem(g + d, n_groups) * rank, rank), rank)

    def fill_group(d):
        fill_kernel(grp_src[cousin_rows(d)], grp_tgt[...], kg_hi.at[d - 1], kg_lo.at[d - 1], 0, 0)

    repeat(n_groups, fill_group)
    fill_kernel(grp_src[own_rows], blk_tgt[...], kd_hi, kd_lo, 0, 0)
    for i in range(leaf_count):
        fill_kernel(blk_src, leaf_tgt[:, rank_cols(i)], kc_hi, kc_lo, 0, i * rank)
        fill_kernel(leaf_src[rank_cols(i)], own_tgt[:, leaf_cols(i)], kt_hi, kt_lo, i * rank, 0)

    for j, c in enumerate(peers):
        up_copy(j, c, c[1]).wait_recv()

    gw = up_out[pl.ds(core, 1)][0]
    for j, c in enumerate(peers):
        gw = gw + up_in[pl.ds(c[1], 1)][0]
    gw_out[...] = gw
    gw_copies = [gw_copy(k, who, g, core) for k, who in enumerate(cousins)]
    for c in gw_copies:
        c.start()

    empty = jnp.zeros((vectors, rank), f32)

    def fill_peer(d):
        src, _ = features(bw_all[lax.rem(m + d, n_blocks)][vectors:])
        fill_kernel(src.T.astype(bf16), blk_tgt[...], kb_hi.at[d - 1], kb_lo.at[d - 1], 0, 0)

    def add_peer(d, acc):
        v2 = split_rows(bw_all[lax.rem(m + d, n_blocks)][:vectors])
        return acc + times_kernel(v2, kb_hi[d - 1], kb_lo[d - 1])


    def halo(there, copies, pts, chg, pad, base):
        @pl.when(there)
        def _():
            for c in copies:
                c.wait_recv()

        @pl.when(jnp.logical_not(there))
        def _():
            pts[...] = jnp.zeros_like(pts)
            chg[...] = jnp.zeros_like(chg)

        src, _ = doubled(pad, pts[0:3])
        ext_src[base : base + block_pts] = src.T.astype(bf16)
        ext_c[:, base : base + block_pts] = chg[...]

    halo(has_left, to_right, pts_left, chg_left, pad_left, 0)
    halo(has_right, to_left, pts_right, chg_right, pad_right, 2 * block_pts)
    for i in range(leaf_count):
        base = leaf_count * leaf_size
        before = list(range(i, leaf_count))
        after = list(range(2 * leaf_count, 2 * leaf_count + i + 1))
        split = base + len(before) * leaf_size
        end = split + len(after) * leaf_size
        target = own_tgt[:, leaf_cols(i)]
        fill_kernel(ext_src[i * leaf_size : block_pts], target, kn_hi.at[i], kn_lo.at[i], base, 0)
        fill_kernel(
            ext_src[2 * block_pts : 2 * block_pts + len(after) * leaf_size], target, kn_hi.at[i], kn_lo.at[i], split, 0)
        v2 = joined([values(i, e) for e in before + after])
        near[i] = near[i] + times_kernel(v2, kn_hi[i, base:end], kn_lo[i, base:end])

    forwards = []
    for k, c in enumerate(same_core):
        bw_copy(0, twin, c).wait_recv()
        forwards.append(bw_copy(1 + len(same_core) + k, twin, c))
        forwards[-1].start()

    repeat(n_blocks // 2, lambda k: fill_peer(2 * k))
    bw_copy(0, twin, twin).wait_recv()
    for c in same_core:
        bw_copy(0, twin, lax.rem(c + twin - m + n_blocks, n_blocks)).wait_recv()
    repeat(n_blocks // 2 + 1, lambda k: fill_peer(2 * k - 1))
    field = gather_terms(n_blocks, add_peer, empty) * scale((n_blocks - 1) * rank)
    @pl.when(has_right)
    def _():
        for c in to_right:
            c.wait_send()

    @pl.when(has_left)
    def _():
        for c in to_left:
            c.wait_send()

    for c in up_copies + bw_copies + forwards + gw_copies:
        c.wait_send()

    for d in range(1, n_groups):
        for part in range(2):
            gw_copy(0, cousins[0], lax.rem(g + d, n_groups), part).wait_recv()

    def add_group(d, acc):
        h = lax.rem(g + d, n_groups)
        v2 = split_rows(jnp.concatenate([gw_all[h, 0], gw_all[h, 1]], axis=0))
        return acc + times_kernel(v2, kg_hi[d - 1], kg_lo[d - 1])

    gfield = gather_terms(n_groups, add_group, empty) * scale((n_groups - 1) * rank)
    field = field + scale(rank) * times_kernel(split_rows(gfield), kd_hi[...], kd_lo[...])
    lf = times_kernel(split_rows(field), kc_hi[...], kc_lo[...]) * scale(rank)
    for i in range(leaf_count):
        far = times_kernel(split_rows(lf[:, rank_cols(i)]), kt_hi[rank_cols(i)], kt_lo[rank_cols(i)])
        out[:, leaf_cols(i)] = near[i] * scale(leaf_size) + far * scale(rank)


def body(n_groups, n_blocks, points, charges, morton, neighbours, counts, skel_leaf, skel_block, skel_group):
    vectors, block_pts = charges.shape
    leaf_count = counts.shape[0]
    leaf_size = block_pts // leaf_count
    rank = skel_block.shape[1]
    slots = neighbours.shape[1]
    leaf_cols = leaf_count * rank
    window = (2 * leaf_count + 1) * leaf_size
    dma = pltpu.SemaphoreType.DMA
    morton = morton.reshape(1, block_pts)
    operands = (points, charges, morton, neighbours, counts, skel_leaf, skel_block, skel_group)
    places = (pltpu.VMEM,) * 3 + (pltpu.SMEM,) * 2 + (pltpu.VMEM,) * 3
    both = lambda *shape: [pltpu.VMEM(shape, bf16)] * 2
    return pl.pallas_call(
        functools.partial(kernel, n_groups, n_blocks, leaf_count, leaf_size, rank, slots),
        out_shape=jax.ShapeDtypeStruct((vectors, block_pts), f32),
        in_specs=[pl.BlockSpec(memory_space=pltpu.HBM)] * len(operands),
        out_specs=pl.BlockSpec(memory_space=pltpu.VMEM),
        scratch_shapes=[
            *[place(a.shape, a.dtype) for place, a in zip(places, operands)],
            pltpu.VMEM((ROWS, block_pts), f32),
            pltpu.VMEM((ROWS, leaf_cols), f32),
            pltpu.VMEM((ROWS, n_groups * rank), f32),
            pltpu.VMEM((ROWS, rank), f32),
            pltpu.VMEM((ROWS, rank), f32),
            pltpu.VMEM((ROWS, block_pts), f32),
            pltpu.VMEM((ROWS, block_pts), f32),
            pltpu.VMEM((ROWS, block_pts), f32),
            pltpu.VMEM((vectors, block_pts), f32),
            pltpu.VMEM((vectors, block_pts), f32),
            pltpu.VMEM((vectors, block_pts), f32),
            pltpu.VMEM((SENT, block_pts), f32),
            pltpu.VMEM((SENT, block_pts), f32),
            pltpu.VMEM((SENT, block_pts), f32),
            pltpu.VMEM((2, vectors // 2, rank), f32),
            pltpu.VMEM((n_blocks, vectors // 2, rank), f32),
            pltpu.VMEM((n_blocks, vectors + ROWS, rank), f32),
            pltpu.VMEM((vectors // 2, rank), f32),
            pltpu.VMEM((n_groups, 2, vectors // 2, rank), f32),
            pltpu.VMEM((3 * block_pts, FEAT), bf16),
            pltpu.VMEM((vectors, 3 * block_pts), f32),
            pltpu.VMEM((FEAT, block_pts), bf16),
            pltpu.VMEM((leaf_cols, FEAT), bf16),
            pltpu.VMEM((FEAT, leaf_cols), bf16),
            pltpu.VMEM((n_groups * rank, FEAT), bf16),
            pltpu.VMEM((FEAT, rank), bf16),
            pltpu.VMEM((FEAT, rank), bf16),
            *both(block_pts, rank),
            *both(leaf_cols, rank),
            *both(rank, rank),
            *both(n_blocks - 1, rank, rank),
            *both(n_groups - 1, rank, rank),
            *both(leaf_count, window, leaf_size),
            *both(rank, rank),
            *both(rank, leaf_cols),
            *both(leaf_cols, leaf_size),
            dma((len(operands),)),
            dma((4,)),
            dma((4,)),
            dma((n_blocks - 1,)),
            dma((n_blocks,)),
            dma((n_blocks,)),
            dma((n_blocks,)),
            dma((2 * (n_groups - 1),)),
            dma((n_groups, 2)),
        ],
        compiler_params=pltpu.CompilerParams(
            collective_id=0, has_side_effects=True, vmem_limit_bytes=64 * 1024 * 1024
        ),
    )(*operands)


def solution(mesh):
    return jax.shard_map(
        functools.partial(body, mesh.shape["grp"], mesh.shape["dev"]),
        mesh=mesh,
        in_specs=(
            P(None, ("grp", "dev")),
            P(None, ("grp", "dev")),
            P(("grp", "dev")),
            P(("grp", "dev"), None),
            P(("grp", "dev")),
            P(None, ("grp", "dev")),
            P(None, ("grp", "dev")),
            P(),
        ),
        out_specs=P(None, ("grp", "dev")),
        check_vma=False,
    )
```

```python
import functools
import math

import jax
import jax.numpy as jnp
from jax import lax
from jax.experimental import pallas as pl
from jax.experimental.pallas import tpu as pltpu
from jax.sharding import PartitionSpec as P

width_sq = 0.1
gain_factor = 5.0
to_base_two = math.sqrt(math.log2(math.e) / width_sq)
middle = 1.0
FEAT = 32
ROWS = 8
SENT = 4
MESH = pl.DeviceIdType.MESH
f32, bf16 = jnp.float32, jnp.bfloat16


def parts(x, count):
    out = []
    for _ in range(count - 1):
        out.append(x.astype(bf16).astype(f32))
        x = x - out[-1]
    out.append(x.astype(bf16).astype(f32))
    return out


def features(coords):
    row = lax.broadcasted_iota(jnp.int32, coords.shape, 0)
    low, used = row < 3, row < 6
    c = jnp.where(used, (coords - middle) * to_base_two, 0.0)
    norm = jnp.sum(jnp.where(low, c * c, 0.0), axis=0, keepdims=True)
    norm = jnp.broadcast_to(norm, c.shape)
    hi, mid, lo = parts(c, 3)
    n0, n1, n2 = parts(norm, 3)
    nth = jnp.where((row == 0) | (row == 3), n0, jnp.where((row == 1) | (row == 4), n1, n2))
    src_n = jnp.where(low, nth, jnp.where(used, 1.0, 0.0))
    tgt_n = jnp.where(low, -1.0, jnp.where(used, -nth, 0.0))
    upper = jnp.where(low, hi + hi, mid + mid)
    src = jnp.concatenate([hi, mid, jnp.where(low, hi, lo), src_n], axis=0)
    tgt = jnp.concatenate([upper, upper, jnp.where(low, lo + lo, hi + hi), tgt_n], axis=0)
    return src, tgt


def split_rows(v):
    return jnp.concatenate(parts(v, 2), axis=0).astype(bf16)


CHUNK = 64


def fill_kernel(src, tgt, k_hi, k_lo, row, col):
    for r in range(0, src.shape[0], CHUNK):
        k = jnp.exp2(jnp.dot(src[r : r + CHUNK], tgt, preferred_element_type=f32))
        hi = k.astype(bf16)
        at = (slice(row + r, row + r + CHUNK), slice(col, col + tgt.shape[1]))
        k_hi[at] = hi
        k_lo[at] = (k - hi.astype(f32)).astype(bf16)


def times_kernel(v2, k_hi, k_lo):
    half = v2.shape[0] // 2
    r = jnp.dot(v2, k_hi, preferred_element_type=f32)
    q = jnp.dot(v2[:half], k_lo, preferred_element_type=f32)
    return r[:half] + r[half:] + q


def repeat(number, step):
    if number <= 8:
        for index in range(1, number):
            step(index)
    else:
        lax.fori_loop(1, number, lambda index, carry: (step(index), carry)[1], 0)


def gather_terms(number, step, start):
    if number <= 8:
        for index in range(1, number):
            start = step(index, start)
        return start
    return lax.fori_loop(1, number, step, start)


def kernel(
    n_groups, n_blocks, leaf_count, leaf_size, rank, slots,
    points_in, charges_in, morton_in, neighbours_in, counts_in, skel_leaf_in, skel_block_in, skel_group_in,
    out,
    points, charges, morton, neighbours, counts, skel_leaf, skel_block, skel_group,
    pad_pts, pad_leaf, pad_grp, pad_own, pad_blk, pad_left, pad_right, sorted_pts, chg_out, chg_left, chg_right,
    pts_out, pts_left, pts_right, up_out, up_in, bw_all, gw_out, gw_all,
    ext_src, ext_c, own_tgt, leaf_src, leaf_tgt, grp_src, grp_tgt, blk_tgt,
    kp_hi, kp_lo, kl_hi, kl_lo, kr_hi, kr_lo, kb_hi, kb_lo, kg_hi, kg_lo, kn_hi, kn_lo,
    kd_hi, kd_lo, kc_hi, kc_lo, kt_hi, kt_lo,
    in_sem, halo_send, halo_recv, up_send, up_recv, bw_send, bw_recv, gw_send, gw_recv,
):
    vectors, block_pts = charges.shape
    g = lax.axis_index("grp")
    m = lax.axis_index("dev")
    block = g * n_blocks + m
    total = n_groups * n_blocks
    right = lax.rem(block + 1, total)
    left = lax.rem(block + total - 1, total)
    right_id = (right // n_blocks, lax.rem(right, n_blocks))
    left_id = (left // n_blocks, lax.rem(left, n_blocks))
    peers = [(g, lax.rem(m + d, n_blocks)) for d in range(1, n_blocks)]
    core = lax.rem(m, 2)
    twin = m + 1 - 2 * core
    same_core = [lax.rem(m + 2 * d, n_blocks) for d in range(1, n_blocks // 2)]
    cousins = [(lax.rem(g + d, n_groups), who) for d in range(1, n_groups) for who in (m, twin)]
    half = vectors // 2

    barrier = pltpu.get_barrier_semaphore()
    greeted = [left_id, right_id] + peers + cousins
    for who in greeted:
        pl.semaphore_signal(barrier, inc=1, device_id=who, device_id_type=MESH)

    pairs = [
        (skel_block_in, skel_block), (skel_leaf_in, skel_leaf), (skel_group_in, skel_group), (morton_in, morton),
        (points_in, points), (charges_in, charges), (neighbours_in, neighbours), (counts_in, counts),
    ]
    loads = [pltpu.make_async_copy(a, b, in_sem.at[k]) for k, (a, b) in enumerate(pairs)]
    for c in loads:
        c.start()

    def scale(terms):
        return gain_factor / math.sqrt(terms)

    def leaf_cols(i):
        return slice(i * leaf_size, (i + 1) * leaf_size)

    def rank_cols(i):
        return slice(i * rank, (i + 1) * rank)

    def doubled(pad, coords):
        pad[6:8] = jnp.zeros((2, coords.shape[1]), f32)
        pad[0:3] = coords
        pad[3:6] = coords
        return features(pad[...])

    for c in loads:
        c.wait()
    pad_pts[6:8] = jnp.zeros((2, block_pts), f32)
    pad_pts[0:3] = points[...]
    pad_pts[3:6] = points[...]
    pts = pad_pts[...]
    stacked = jnp.concatenate(
        parts(pts, 3) + [jnp.zeros_like(pts)] + parts(charges[...], 2), axis=0
    ).astype(bf16)
    place = lax.broadcasted_iota(jnp.int32, (leaf_size, leaf_size), 0)
    for i in range(leaf_count):
        s = jnp.zeros((stacked.shape[0], leaf_size), f32)
        for r in range(0, block_pts, leaf_size):
            onehot = jnp.where(place == morton[0:1, leaf_cols(i)] - r, 1.0, 0.0).astype(bf16)
            s = s + jnp.dot(stacked[:, r : r + leaf_size], onehot, preferred_element_type=f32)
        sorted_pts[:, leaf_cols(i)] = s[0:8] + s[8:16] + s[16:24]
        chg_out[:, leaf_cols(i)] = s[32 : 32 + vectors] + s[32 + vectors :]
    pts_out[...] = sorted_pts[0:SENT]

    def to_peer(src, dst, send, recv, who):
        return pltpu.make_async_remote_copy(
            src_ref=src, dst_ref=dst, send_sem=send, recv_sem=recv, device_id=who, device_id_type=MESH)

    to_right = [
        to_peer(pts_out, pts_left, halo_send.at[0], halo_recv.at[0], right_id),
        to_peer(chg_out, chg_left, halo_send.at[1], halo_recv.at[1], right_id),
    ]
    to_left = [
        to_peer(pts_out, pts_right, halo_send.at[2], halo_recv.at[2], left_id),
        to_peer(chg_out, chg_right, halo_send.at[3], halo_recv.at[3], left_id),
    ]
    has_left, has_right = block > 0, block < total - 1

    pl.semaphore_wait(barrier, len(greeted))

    @pl.when(has_right)
    def _():
        for c in to_right:
            c.start()

    @pl.when(has_left)
    def _():
        for c in to_left:
            c.start()

    own_rows = pl.ds(pl.multiple_of(g * rank, rank), rank)
    src_b, tgt = doubled(pad_blk, skel_block[...])
    bw_all[pl.ds(m, 1), vectors:] = pad_blk[...][None]
    blk_tgt[...] = tgt.astype(bf16)
    blk_src = src_b.T.astype(bf16)
    src, tgt = doubled(pad_leaf, skel_leaf[...])
    leaf_src[...] = src.T.astype(bf16)
    leaf_tgt[...] = tgt.astype(bf16)
    _, tgt = doubled(pad_own, skel_group[:, own_rows])
    grp_tgt[...] = tgt.astype(bf16)
    fill_kernel(leaf_src[...], blk_tgt[...], kl_hi, kl_lo, 0, 0)
    fill_kernel(blk_src, grp_tgt[...], kr_hi, kr_lo, 0, 0)

    src, tgt = features(sorted_pts[...])
    ext_src[block_pts : 2 * block_pts] = src.T.astype(bf16)
    own_tgt[...] = tgt.astype(bf16)
    leaf_w = []
    for i in range(leaf_count):
        fill_kernel(ext_src[leaf_cols(leaf_count + i)], leaf_tgt[:, rank_cols(i)], kp_hi, kp_lo, i * leaf_size, 0)
        leaf_w.append(times_kernel(split_rows(chg_out[:, leaf_cols(i)]), kp_hi[leaf_cols(i)], kp_lo[leaf_cols(i)]))
    lw = jnp.concatenate(leaf_w, axis=1) * scale(leaf_size)
    bw = times_kernel(split_rows(lw), kl_hi[...], kl_lo[...]) * scale(leaf_count * rank)
    bw_all[pl.ds(m, 1), 0:vectors] = bw[None]
    up = times_kernel(split_rows(bw), kr_hi[...], kr_lo[...]) * scale(n_blocks * rank)
    up_out[0] = up[:half]
    up_out[1] = up[half:]

    def up_copy(k, who, slot):
        return to_peer(up_out.at[lax.rem(who[1], 2)], up_in.at[slot], up_send.at[k], up_recv.at[slot], who)

    def bw_copy(k, who, slot):
        return to_peer(bw_all.at[slot], bw_all.at[slot], bw_send.at[k], bw_recv.at[slot], (g, who))

    def gw_copy(k, who, group, part):
        return to_peer(gw_out, gw_all.at[group, part], gw_send.at[k], gw_recv.at[group, part], who)

    up_copies = [up_copy(k, who, m) for k, who in enumerate(peers)]
    bw_copies = [bw_copy(k, who, m) for k, who in enumerate([twin] + same_core)]
    for c in up_copies:
        c.start()

    for c in bw_copies:
        c.start()

    ext_c[:, block_pts : 2 * block_pts] = chg_out[...]
    first_leaf = block * leaf_count - leaf_count

    def values(i, e):
        piece = ext_c[:, leaf_cols(e)]
        if e == leaf_count + i:
            return piece
        times = jnp.int32(0)
        for k in range(slots):
            hit = (neighbours[i, k] - first_leaf == e) & (k < counts[i])
            times = times + jnp.where(hit, 1, 0)
        return piece * times.astype(f32)

    def joined(pieces):
        return split_rows(jnp.concatenate(pieces, axis=1))

    near = []
    for i in range(leaf_count):
        fill_kernel(
            ext_src[block_pts : 2 * block_pts], own_tgt[:, leaf_cols(i)], kn_hi.at[i], kn_lo.at[i], 0, 0)
        v2 = joined([values(i, leaf_count + j) for j in range(leaf_count)])
        near.append(times_kernel(v2, kn_hi[i, 0:block_pts], kn_lo[i, 0:block_pts]))

    src, _ = doubled(pad_grp, skel_group[...])
    grp_src[...] = src.T.astype(bf16)

    def cousin_rows(d):
        return pl.ds(pl.multiple_of(lax.rem(g + d, n_groups) * rank, rank), rank)

    def fill_group(d):
        fill_kernel(grp_src[cousin_rows(d)], grp_tgt[...], kg_hi.at[d - 1], kg_lo.at[d - 1], 0, 0)

    repeat(n_groups, fill_group)
    fill_kernel(grp_src[own_rows], blk_tgt[...], kd_hi, kd_lo, 0, 0)
    for i in range(leaf_count):
        fill_kernel(blk_src, leaf_tgt[:, rank_cols(i)], kc_hi, kc_lo, 0, i * rank)
        fill_kernel(leaf_src[rank_cols(i)], own_tgt[:, leaf_cols(i)], kt_hi, kt_lo, i * rank, 0)

    for j, c in enumerate(peers):
        up_copy(j, c, c[1]).wait_recv()

    gw = up_out[pl.ds(core, 1)][0]
    for j, c in enumerate(peers):
        gw = gw + up_in[pl.ds(c[1], 1)][0]
    gw_out[...] = gw
    gw_copies = [gw_copy(k, who, g, core) for k, who in enumerate(cousins)]
    for c in gw_copies:
        c.start()

    empty = jnp.zeros((vectors, rank), f32)

    def fill_peer(d):
        src, _ = features(bw_all[lax.rem(m + d, n_blocks)][vectors:])
        fill_kernel(src.T.astype(bf16), blk_tgt[...], kb_hi.at[d - 1], kb_lo.at[d - 1], 0, 0)

    def add_peer(d, acc):
        v2 = split_rows(bw_all[lax.rem(m + d, n_blocks)][:vectors])
        return acc + times_kernel(v2, kb_hi[d - 1], kb_lo[d - 1])


    def halo(there, copies, pts, chg, pad, base):
        @pl.when(there)
        def _():
            for c in copies:
                c.wait_recv()

        @pl.when(jnp.logical_not(there))
        def _():
            pts[...] = jnp.zeros_like(pts)
            chg[...] = jnp.zeros_like(chg)

        src, _ = doubled(pad, pts[0:3])
        ext_src[base : base + block_pts] = src.T.astype(bf16)
        ext_c[:, base : base + block_pts] = chg[...]

    halo(has_left, to_right, pts_left, chg_left, pad_left, 0)
    halo(has_right, to_left, pts_right, chg_right, pad_right, 2 * block_pts)
    for i in range(leaf_count):
        base = leaf_count * leaf_size
        before = list(range(i, leaf_count))
        after = list(range(2 * leaf_count, 2 * leaf_count + i + 1))
        split = base + len(before) * leaf_size
        end = split + len(after) * leaf_size
        target = own_tgt[:, leaf_cols(i)]
        fill_kernel(ext_src[i * leaf_size : block_pts], target, kn_hi.at[i], kn_lo.at[i], base, 0)
        fill_kernel(
            ext_src[2 * block_pts : 2 * block_pts + len(after) * leaf_size], target, kn_hi.at[i], kn_lo.at[i], split, 0)
        v2 = joined([values(i, e) for e in before + after])
        near[i] = near[i] + times_kernel(v2, kn_hi[i, base:end], kn_lo[i, base:end])

    forwards = []
    for k, c in enumerate(same_core):
        bw_copy(0, twin, c).wait_recv()
        forwards.append(bw_copy(1 + len(same_core) + k, twin, c))
        forwards[-1].start()

    repeat(n_blocks // 2, lambda k: fill_peer(2 * k))
    bw_copy(0, twin, twin).wait_recv()
    for c in same_core:
        bw_copy(0, twin, lax.rem(c + twin - m + n_blocks, n_blocks)).wait_recv()
    repeat(n_blocks // 2 + 1, lambda k: fill_peer(2 * k - 1))
    field = gather_terms(n_blocks, add_peer, empty) * scale((n_blocks - 1) * rank)
    @pl.when(has_right)
    def _():
        for c in to_right:
            c.wait_send()

    @pl.when(has_left)
    def _():
        for c in to_left:
            c.wait_send()

    for c in up_copies + bw_copies + forwards + gw_copies:
        c.wait_send()

    for d in range(1, n_groups):
        for part in range(2):
            gw_copy(0, cousins[0], lax.rem(g + d, n_groups), part).wait_recv()

    def add_group(d, acc):
        h = lax.rem(g + d, n_groups)
        v2 = split_rows(jnp.concatenate([gw_all[h, 0], gw_all[h, 1]], axis=0))
        return acc + times_kernel(v2, kg_hi[d - 1], kg_lo[d - 1])

    gfield = gather_terms(n_groups, add_group, empty) * scale((n_groups - 1) * rank)
    field = field + scale(rank) * times_kernel(split_rows(gfield), kd_hi[...], kd_lo[...])
    lf = times_kernel(split_rows(field), kc_hi[...], kc_lo[...]) * scale(rank)
    for i in range(leaf_count):
        far = times_kernel(split_rows(lf[:, rank_cols(i)]), kt_hi[rank_cols(i)], kt_lo[rank_cols(i)])
        out[:, leaf_cols(i)] = near[i] * scale(leaf_size) + far * scale(rank)


def body(n_groups, n_blocks, points, charges, morton, neighbours, counts, skel_leaf, skel_block, skel_group):
    vectors, block_pts = charges.shape
    leaf_count = counts.shape[0]
    leaf_size = block_pts // leaf_count
    rank = skel_block.shape[1]
    slots = neighbours.shape[1]
    leaf_cols = leaf_count * rank
    window = (2 * leaf_count + 1) * leaf_size
    dma = pltpu.SemaphoreType.DMA
    morton = morton.reshape(1, block_pts)
    operands = (points, charges, morton, neighbours, counts, skel_leaf, skel_block, skel_group)
    places = (pltpu.VMEM,) * 3 + (pltpu.SMEM,) * 2 + (pltpu.VMEM,) * 3
    both = lambda *shape: [pltpu.VMEM(shape, bf16)] * 2
    return pl.pallas_call(
        functools.partial(kernel, n_groups, n_blocks, leaf_count, leaf_size, rank, slots),
        out_shape=jax.ShapeDtypeStruct((vectors, block_pts), f32),
        in_specs=[pl.BlockSpec(memory_space=pltpu.HBM)] * len(operands),
        out_specs=pl.BlockSpec(memory_space=pltpu.VMEM),
        scratch_shapes=[
            *[place(a.shape, a.dtype) for place, a in zip(places, operands)],
            pltpu.VMEM((ROWS, block_pts), f32),
            pltpu.VMEM((ROWS, leaf_cols), f32),
            pltpu.VMEM((ROWS, n_groups * rank), f32),
            pltpu.VMEM((ROWS, rank), f32),
            pltpu.VMEM((ROWS, rank), f32),
            pltpu.VMEM((ROWS, block_pts), f32),
            pltpu.VMEM((ROWS, block_pts), f32),
            pltpu.VMEM((ROWS, block_pts), f32),
            pltpu.VMEM((vectors, block_pts), f32),
            pltpu.VMEM((vectors, block_pts), f32),
            pltpu.VMEM((vectors, block_pts), f32),
            pltpu.VMEM((SENT, block_pts), f32),
            pltpu.VMEM((SENT, block_pts), f32),
            pltpu.VMEM((SENT, block_pts), f32),
            pltpu.VMEM((2, vectors // 2, rank), f32),
            pltpu.VMEM((n_blocks, vectors // 2, rank), f32),
            pltpu.VMEM((n_blocks, vectors + ROWS, rank), f32),
            pltpu.VMEM((vectors // 2, rank), f32),
            pltpu.VMEM((n_groups, 2, vectors // 2, rank), f32),
            pltpu.VMEM((3 * block_pts, FEAT), bf16),
            pltpu.VMEM((vectors, 3 * block_pts), f32),
            pltpu.VMEM((FEAT, block_pts), bf16),
            pltpu.VMEM((leaf_cols, FEAT), bf16),
            pltpu.VMEM((FEAT, leaf_cols), bf16),
            pltpu.VMEM((n_groups * rank, FEAT), bf16),
            pltpu.VMEM((FEAT, rank), bf16),
            pltpu.VMEM((FEAT, rank), bf16),
            *both(block_pts, rank),
            *both(leaf_cols, rank),
            *both(rank, rank),
            *both(n_blocks - 1, rank, rank),
            *both(n_groups - 1, rank, rank),
            *both(leaf_count, window, leaf_size),
            *both(rank, rank),
            *both(rank, leaf_cols),
            *both(leaf_cols, leaf_size),
            dma((len(operands),)),
            dma((4,)),
            dma((4,)),
            dma((n_blocks - 1,)),
            dma((n_blocks,)),
            dma((n_blocks,)),
            dma((n_blocks,)),
            dma((2 * (n_groups - 1),)),
            dma((n_groups, 2)),
        ],
        compiler_params=pltpu.CompilerParams(
            collective_id=0, has_side_effects=True, vmem_limit_bytes=64 * 1024 * 1024
        ),
    )(*operands)


def solution(mesh):
    return jax.shard_map(
        functools.partial(body, mesh.shape["grp"], mesh.shape["dev"]),
        mesh=mesh,
        in_specs=(
            P(None, ("grp", "dev")),
            P(None, ("grp", "dev")),
            P(("grp", "dev")),
            P(("grp", "dev"), None),
            P(("grp", "dev")),
            P(None, ("grp", "dev")),
            P(None, ("grp", "dev")),
            P(),
        ),
        out_specs=P(None, ("grp", "dev")),
        check_vma=False,
    )
```
